128 devices in a mesh: seq: 8 (over z, core), enc: 16 (over x, y).
Axes of the slice: x: 4, y: 4, z: 4, core: 2. Of those that a mesh axis runs over, the one named last changes fastest.
Arguments:
- queries: bfloat16 [16384, 4096], P(('seq', 'enc')), may hold values from -8 to 8
- keys: bfloat16 [16, 1601, 512], P('enc'), may hold values from -8 to 8
- values: bfloat16 [16, 1601, 512], P('enc'), may hold values from -24 to 24
- reads: int32 [128, 8], replicated, may hold values from 0 to 15, all different within a row; in each aligned block of 16 rows (0 to 15, 16 to 31, ...) at most 12 rows name the same one
- grad_out: bfloat16 [16384, 4096], P(('seq', 'enc')), may hold values from -24 to 24
Outputs:
- attended: bfloat16 [16384, 4096], P(('seq', 'enc'))
- grad_queries: bfloat16 [16384, 4096], P(('seq', 'enc'))
- grad_keys: bfloat16 [16, 1601, 512], P('enc', None, 'seq')
- grad_values: bfloat16 [16, 1601, 512], P('enc', None, 'seq')
The draws below stay inside these ranges and needn't reach their ends.
Inputs may be any that keep to these rules, and one draw needn't show every extreme that they name: `reads`: each row names 8 different images; in each aligned block of 16 rows (the text blocks of one index of seq) no image is named by more than 12 rows, and in some such block one image is named by exactly 12.
All inputs are finite; a program needn't handle non-finite values.
Results may differ from the reference program's by a relative error of at most 0.04.
Values may be sent and summed in bfloat16 or wider, within the bound.
A program may use at most 128 MiB of HBM per device.

```python
import math
import jax
import jax.numpy as jnp
import numpy as np
from jax import lax

HQ = 32
KVH = 4
HD = 128
VT = 1601
R = 8
MOST = 12
SEG = 16
IMAGES = 16
BLOCKS = 128
TOKENS = 16384
N_SEQ = 8
N_ENC = 16


def draw_queries(key, part):
    key = jax.random.fold_in(key, 11)
    base = jnp.clip(jax.random.normal(key, (TOKENS, HQ * HD), jnp.float32), -6.0, 6.0)
    return base.astype(jnp.bfloat16)


def draw_keys(key, part):
    key = jax.random.fold_in(key, 12)
    base = jnp.clip(jax.random.normal(key, (IMAGES, VT, KVH * HD), jnp.float32), -6.0, 6.0)
    return base.astype(jnp.bfloat16)


def shard_levels(key, extent, cuts, smallest, largest):
    def one(dim, shards_of):
        draws = jax.random.uniform(jax.random.fold_in(jax.random.fold_in(key, 6), dim), (shards_of,), jnp.float32, smallest / len(cuts), largest / len(cuts))
        return jnp.repeat(jnp.exp(draws), extent[dim] // shards_of).reshape((-1,) + (1,) * (len(extent) - dim - 1))

    gain = one(*cuts[0])
    for cut in cuts[1:]:
        gain = gain * one(*cut)
    return gain


def assign_block(stream_key, own, number, rows, amount, top, bound, lean):
    ranking = jax.random.permutation(stream_key, amount)
    heavy_load, common = shares(amount, rows * top, bound, lean, True), shares(amount, rows * top, bound, lean, False)
    places = jnp.arange(amount)

    def named(lengths, turn):
        used = int((lengths > 0).sum())
        fixed = max(1, used // 4)
        moved = fixed + (places - fixed + turn * (used - fixed)) % max(1, amount - fixed)
        return jnp.zeros((amount,), jnp.int32).at[ranking[jnp.where(places < fixed, places, moved)]].set(jnp.asarray(lengths, jnp.int32))

    lengths = jnp.where(number % 4 == 0, named(heavy_load, number // 4), named(common, number - number // 4 - 1))
    mixed = jax.random.permutation(jax.random.fold_in(own, 3), amount)
    source_of, receiver = mixed[0:amount // 2 * 2:2], mixed[1:amount // 2 * 2:2]
    room = jnp.minimum(lengths[source_of] - 1, bound - lengths[receiver]) // 2
    room = jnp.where((source_of == ranking[0]) | (receiver == ranking[0]) | (lengths[receiver] == 0), 0, jnp.maximum(room, 0))
    moved = jax.random.randint(jax.random.fold_in(own, 4), (amount // 2,), 0, 1 << 20) % (room + 1)
    lengths = lengths.at[source_of].add(-moved).at[receiver].add(moved)
    labels = jnp.searchsorted(jnp.cumsum(lengths), jnp.arange(rows * top), side="right").astype(jnp.int32)
    table = labels.reshape(top, rows).T
    table = table[jax.random.permutation(jax.random.fold_in(own, 1), rows)]
    turn = jax.random.randint(jax.random.fold_in(own, 2), (rows, 1), 0, top)
    return jnp.take_along_axis(table, (jnp.arange(top)[None, :] + turn) % top, axis=1)


def shares(count, total, most, lean, full):
    weights = [(1 << 20) // math.isqrt(grade ** lean) + 1 for grade in range(1, count + 1)]
    largest = most if full else min(most, max(-(-total // count), total * weights[0] // sum(weights)))
    least = 1 if total - largest >= count - 1 else 0
    counts, surplus = [largest] + [least] * (count - 1), total - largest - least * (count - 1)
    while surplus > 0:
        free = [i for i in range(1, count) if counts[i] < largest] or [i for i in range(1, count) if counts[i] < most]
        pool, remaining = sum([weights[i] for i in free]), surplus
        for i in free:
            extra = min(most - counts[i], max(1, remaining * weights[i] // pool), surplus)
            counts[i] = counts[i] + extra
            surplus = surplus - extra
    return np.array(counts)


def bell_draw(key, shape, deviation, most, cuts=(), kind=jnp.bfloat16):
    level = shard_levels(key, shape, cuts, -0.22, 0.18) if cuts else 1.0
    drawn = jax.random.normal(key, shape, jnp.float32) * deviation * level
    return jnp.minimum(jnp.maximum(drawn, -most), most).astype(kind)


def setup_inputs(seed: int = 0) -> dict:
    key_list = jax.random.split(jax.random.key(seed), 6)
    queries = draw_queries(jax.random.fold_in(key_list[5], 71), 0)
    keys = draw_keys(jax.random.fold_in(key_list[5], 71), 0)
    values = bell_draw(key_list[2], (IMAGES, VT, KVH * HD), 4.0, 24.0, ((0, 16),))
    reads_keys = jax.random.split(jax.random.fold_in(key_list[3], 1), BLOCKS // N_ENC)
    reads_turns = jax.random.permutation(jax.random.fold_in(key_list[3], 3), BLOCKS // N_ENC)
    reads = jax.vmap(lambda own, number: assign_block(jax.random.fold_in(key_list[3], 2), own, number, N_ENC, IMAGES, R, MOST, 2))(reads_keys, reads_turns).reshape((BLOCKS, R))
    grad_out = bell_draw(key_list[4], (TOKENS, HQ * HD), 4.0, 24.0, ((0, 128),))
    return {"queries": queries, "keys": keys, "values": values, "reads": reads, "grad_out": grad_out}


def forward_heads(rows_q, keys_img, values_img):
    count = rows_q.shape[0]
    group = HQ // KVH
    scale = HD ** -0.5
    outputs = []
    totals = []
    for head in range(KVH):
        q_head = rows_q[:, head * group * HD:(head + 1) * group * HD].reshape(count, group, HD).astype(jnp.float32)
        k_head = keys_img[:, head * HD:(head + 1) * HD].astype(jnp.float32)
        v_head = values_img[:, head * HD:(head + 1) * HD].astype(jnp.float32)
        scores = jnp.einsum("ngd,jd->ngj", q_head, k_head) * scale
        top = jnp.max(scores, axis=-1, keepdims=True)
        total = jnp.sum(jnp.exp(scores - top), axis=-1, keepdims=True)
        lse = top + jnp.log(total)
        weights = jnp.exp(scores - lse).astype(jnp.bfloat16)
        output = jnp.einsum("ngj,jd->ngd", weights.astype(jnp.float32), v_head)
        outputs.append(output.reshape(count, group * HD))
        totals.append(lse[..., 0])
    return jnp.concatenate(outputs, axis=-1).astype(jnp.bfloat16), jnp.stack(totals, axis=1)


def backward_heads(rows_q, rows_o, rows_g, lse_all, keys_img, values_img):
    count = rows_q.shape[0]
    group = HQ // KVH
    scale = HD ** -0.5
    query_parts = []
    key_parts = []
    value_parts = []
    for head in range(KVH):
        cols = slice(head * group * HD, (head + 1) * group * HD)
        q_head = rows_q[:, cols].reshape(count, group, HD).astype(jnp.float32)
        o_head = rows_o[:, cols].reshape(count, group, HD).astype(jnp.float32)
        g_head = rows_g[:, cols].reshape(count, group, HD).astype(jnp.float32)
        k_head = keys_img[:, head * HD:(head + 1) * HD].astype(jnp.float32)
        v_head = values_img[:, head * HD:(head + 1) * HD].astype(jnp.float32)
        scores = jnp.einsum("ngd,jd->ngj", q_head, k_head) * scale
        prob = jnp.exp(scores - lse_all[:, head][..., None])
        weights = prob.astype(jnp.bfloat16).astype(jnp.float32)
        delta = jnp.sum(g_head * o_head, axis=-1)
        dprob = jnp.einsum("ngd,jd->ngj", g_head, v_head)
        dscore = (prob * (dprob - delta[..., None])).astype(jnp.bfloat16).astype(jnp.float32)
        query_parts.append((jnp.einsum("ngj,jd->ngd", dscore, k_head) * scale).reshape(count, group * HD))
        key_parts.append(jnp.einsum("ngj,ngd->jd", dscore, q_head) * scale)
        value_parts.append(jnp.einsum("ngj,ngd->jd", weights, g_head))
    grad_rows = jnp.concatenate(query_parts, axis=-1).astype(jnp.bfloat16)
    return grad_rows, jnp.concatenate(key_parts, axis=-1), jnp.concatenate(value_parts, axis=-1)


def reference(queries, keys, values, reads, grad_out):
    width = HQ * HD
    span = KVH * HD
    q_rows = queries.reshape(N_SEQ, N_ENC, R, SEG, width)
    g_rows = grad_out.reshape(N_SEQ, N_ENC, R, SEG, width)
    r_rows = reads.reshape(N_SEQ, N_ENC, R)
    empty = jnp.zeros((IMAGES, VT, span), jnp.float32)

    def one_block(carry, item):
        key_sum, value_sum = carry
        q_block, g_block, r_block = item
        outputs = []
        grads = []
        for segment in range(R):
            image = r_block[segment].astype(jnp.int32)
            key_img = lax.dynamic_index_in_dim(keys, image, 0, keepdims=False)
            value_img = lax.dynamic_index_in_dim(values, image, 0, keepdims=False)
            output, lse_all = forward_heads(q_block[segment], key_img, value_img)
            grad_rows, key_part, value_part = backward_heads(q_block[segment], output, g_block[segment], lse_all, key_img, value_img)
            key_sum = key_sum.at[image].add(key_part)
            value_sum = value_sum.at[image].add(value_part)
            outputs.append(output)
            grads.append(grad_rows)
        return (key_sum, value_sum), (jnp.stack(outputs), jnp.stack(grads))

    def one_row(carry, item):
        total_keys, total_values = carry
        (row_keys, row_values), (outputs, grads) = lax.scan(one_block, (empty, empty), item)
        total_keys = total_keys + lax.optimization_barrier(row_keys.astype(jnp.bfloat16)).astype(jnp.float32)
        total_values = total_values + lax.optimization_barrier(row_values.astype(jnp.bfloat16)).astype(jnp.float32)
        return (total_keys, total_values), (outputs, grads)

    (total_keys, total_values), (outputs, grads) = lax.scan(one_row, (empty, empty), (q_rows, g_rows, r_rows))
    attended = outputs.reshape(TOKENS, width)
    grad_queries = grads.reshape(TOKENS, width)
    return attended, grad_queries, total_keys.astype(jnp.bfloat16), total_values.astype(jnp.bfloat16)
```

```python
import functools

import jax
import jax.numpy as jnp
from jax import lax
from jax.experimental import pallas as pl
from jax.experimental.pallas import tpu as pltpu
from jax.sharding import PartitionSpec as P

HQ = 32
KVH = 4
HD = 128
GROUP = HQ // KVH
SEG = 16
ROWS = GROUP * SEG
VT = 1601
VT16 = 1616
JP = 1664
LOG2E = 1.4426950408889634
MESH = pl.DeviceIdType.MESH
BF16 = jnp.bfloat16
F32 = jnp.float32
CHUNKS = [(j, min(256, JP - j)) for j in range(0, JP, 256)]
NT = (((1,), (1,)), ((), ()))
T_SEND, T_SRC, T_OK, T_POS, T_READ = 0, 16, 32, 48, 64


def kernel(
    slots, tab, q_in, g_in, k_in, v_in, att_out, gq_out, gk_out, gv_out,
    a_q, a_g, a_o, a_d, m_q, m_g, m_o, m_d, r_q, r_g, r_o, r_d,
    kh, vh, kt, vt, stage_q, stage_g, pack_o, pack_d, s_scr, p_scr, k_acc, v_acc,
    z_send, z_recv, c_send, c_recv,
    s1, w1, s2, w2, zs, zw, cs, cw,
):
    sq = lax.axis_index("seq")
    en = lax.axis_index("enc")
    z, core = sq // 2, sq % 2
    x, y = en // 4, en % 4
    scale = HD ** (-0.5)

    first = (a_q, a_g, a_o, a_d)
    middle = (m_q, m_g, m_o, m_d)
    last = (r_q, r_g, r_o, r_d)
    own = [(x, y), (y, x), (x, y), (y, x)]

    def peer(axis, d):
        if axis == 0:
            return (sq, ((x + d) % 4) * 4 + y)
        return (sq, x * 4 + (y + d) % 4)

    def hop1(ten, t, d):
        return pltpu.make_async_remote_copy(
            src_ref=first[ten].at[t, d - 1],
            dst_ref=middle[ten].at[t, :, own[ten][0]],
            send_sem=s1.at[ten, t, d - 1],
            recv_sem=w1.at[ten, t, d - 1],
            device_id=peer(ten % 2, d),
            device_id_type=MESH,
        )

    def hop2(ten, t, d):
        b = own[ten][1]
        return pltpu.make_async_remote_copy(
            src_ref=middle[ten].at[t, (b + d) % 4],
            dst_ref=last[ten].at[t, b],
            send_sem=s2.at[ten, t, d - 1],
            recv_sem=w2.at[ten, t, d - 1],
            device_id=peer(1 - ten % 2, d),
            device_id_type=MESH,
        )

    def start1(pair, t):
        for d in (2, 1, 3):
            for ten in pair:
                hop1(ten, t, d).start()

    def forward(pair, t):
        for ten in pair:
            for d in (1, 2, 3):
                hop1(ten, t, d).wait_recv()
            for d in (2, 1, 3):
                hop2(ten, t, d).start()

    def arrive(pair, t):
        for ten in pair:
            for d in (1, 2, 3):
                hop2(ten, t, d).wait_recv()

    def z_copy(t):
        return pltpu.make_async_remote_copy(
            src_ref=z_send.at[t],
            dst_ref=z_recv.at[t],
            send_sem=zs.at[t],
            recv_sem=zw.at[t],
            device_id=(((z + 1 + t) % 4) * 2 + core, en),
            device_id_type=MESH,
        )

    def head_at(t):
        return (z + 1 + t) % 4

    IN, OUT = (0, 1), (2, 3)

    barrier = pltpu.get_barrier_semaphore()
    for d in (1, 2, 3):
        for target in (peer(0, d), peer(1, d), (((z + d) % 4) * 2 + core, en)):
            pl.semaphore_signal(barrier, inc=1, device_id=target, device_id_type=MESH)
    pl.semaphore_signal(barrier, inc=1, device_id=(z * 2 + 1 - core, en), device_id_type=MESH)

    def pack_in(t):
        cols = pl.ds(pl.multiple_of(head_at(t) * (GROUP * HD), GROUP * HD), GROUP * HD)
        for ten, src in ((0, q_in), (1, g_in)):
            a_own = own[ten][0]
            for d in range(4):
                a = (a_own + d) % 4
                for b in range(4):
                    image = a * 4 + b if ten == 0 else b * 4 + a
                    block = src[tab[T_SEND + image], :, cols]
                    for g in range(GROUP):
                        piece = block[:, g * HD : (g + 1) * HD]
                        rows = pl.ds(g * SEG, SEG)
                        if d == 0:
                            middle[ten][t, b, a_own, rows, :] = piece
                        else:
                            first[ten][t, d - 1, b, rows, :] = piece

    pack_in(0)
    pl.semaphore_wait(barrier, 10)
    start1(IN, 0)
    pack_in(1)
    start1(IN, 1)

    def rest(t, carry):
        pack_in(t)
        return carry

    lax.fori_loop(2, KVH, rest, 0)

    def heads(t, carry):
        cols = pl.ds(pl.multiple_of(head_at(t) * HD, HD), HD)
        for src, rows_ref, cols_ref in ((k_in, kh, kt), (v_in, vh, vt)):
            rows_ref[t, 0:1600, :] = src[0, 0:1600, cols]
            tail = src[0, 1600:VT, cols].astype(F32)
            mark = lax.broadcasted_iota(jnp.int32, (64, HD), 0) == 0
            rows_ref[t, 1600:JP, :] = jnp.where(
                mark, jnp.broadcast_to(tail, (64, HD)), 0.0
            ).astype(BF16)
            for j in range(0, JP, HD):
                cols_ref[t, :, j : j + HD] = rows_ref[t, j : j + HD, :].T
        return carry

    lax.fori_loop(0, KVH, heads, 0)

    forward(IN, 0)
    start1(IN, 2)

    def tile(t, i):
        src0, src1 = tab[T_SRC + 2 * i], tab[T_SRC + 2 * i + 1]
        ok0, ok1 = tab[T_OK + 2 * i], tab[T_OK + 2 * i + 1]
        turned0 = (src0 % 4) * 4 + src0 // 4
        turned1 = (src1 % 4) * 4 + src1 // 4
        q = jnp.concatenate([stage_q[turned0], stage_q[turned1]], axis=0)
        g0 = stage_g[src0].astype(F32)
        g1 = stage_g[src1].astype(F32)
        g_t = jnp.concatenate(
            [jnp.where(ok0 > 0, g0, 0.0).T, jnp.where(ok1 > 0, g1, 0.0).T], axis=1
        )
        top = jnp.full((8, 2 * ROWS), -jnp.inf, F32)
        for j, n in CHUNKS:
            s = lax.dot_general(kh[t, j : j + n, :], q, NT, preferred_element_type=F32)
            if j + n > VT:
                row = lax.broadcasted_iota(jnp.int32, s.shape, 0) + j
                s = jnp.where(row < VT, s, -1e30)
            s_scr[j : j + n, :] = s
            top = jnp.maximum(top, jnp.max(s.reshape(n // 8, 8, 2 * ROWS), axis=0))
        c2 = scale * LOG2E
        top2 = jnp.max(top, axis=0, keepdims=True) * c2
        total = jnp.zeros((8, 2 * ROWS), F32)
        o_t = jnp.zeros((HD, 2 * ROWS), F32)
        for j, n in CHUNKS:
            p = jnp.exp2(s_scr[j : j + n, :] * c2 - top2)
            total += jnp.sum(p.reshape(n // 8, 8, 2 * ROWS), axis=0)
            p_b = p.astype(BF16)
            p_scr[j : j + n, :] = p_b
            o_t += jnp.dot(vt[t, :, j : j + n], p_b, preferred_element_type=F32)
        inv = 1.0 / jnp.sum(total, axis=0, keepdims=True)
        o_t = (o_t * inv).astype(BF16).astype(F32)
        pack_o[2 * i] = o_t[:, :ROWS].T.astype(BF16)
        pack_o[2 * i + 1] = o_t[:, ROWS:].T.astype(BF16)
        delta = jnp.sum(g_t * o_t, axis=0, keepdims=True) * inv
        g_s = (g_t * inv).astype(BF16)
        d_t = jnp.zeros((HD, 2 * ROWS), F32)
        for j, n in CHUNKS:
            dp = jnp.dot(vh[t, j : j + n, :], g_s, preferred_element_type=F32)
            p_b = p_scr[j : j + n, :]
            ds = (p_b.astype(F32) * (dp - delta)).astype(BF16)
            v_acc[j : j + n, :] += lax.dot_general(p_b, g_s, NT, preferred_element_type=F32)
            k_acc[j : j + n, :] += jnp.dot(ds, q, preferred_element_type=F32)
            d_t += jnp.dot(kt[t, :, j : j + n], ds, preferred_element_type=F32)
        d_t = d_t * scale
        pack_d[2 * i] = d_t[:, :ROWS].T.astype(BF16)
        pack_d[2 * i + 1] = d_t[:, ROWS:].T.astype(BF16)

    def step(t, carry):
        arrive(IN, t)
        for ten, stage in ((0, stage_q), (1, stage_g)):
            b_own = own[ten][1]
            for d in range(4):
                b = (b_own + d) % 4
                for a in range(4):
                    if d == 0:
                        stage[b * 4 + a] = middle[ten][t, b, a]
                    else:
                        stage[b * 4 + a] = last[ten][t, b, a]
        k_acc[...] = jnp.zeros_like(k_acc)
        v_acc[...] = jnp.zeros_like(v_acc)

        def one(i, inner):
            tile(t, i)

            @pl.when((i == 0) & (t < KVH - 1))
            def _():
                forward(IN, t + 1)

            @pl.when((i == 0) & (t + 3 < KVH))
            def _():
                start1(IN, t + 3)

            @pl.when((i == 2) & (t > 0))
            def _():
                forward(OUT, t - 1)

            return inner

        lax.fori_loop(0, slots // 2, one, 0)

        for ten, packed in ((2, pack_o), (3, pack_d)):
            a_own = own[ten][0]
            for d in range(4):
                a = (a_own + d) % 4
                for b in range(4):
                    block = a * 4 + b if ten == 2 else b * 4 + a
                    piece = packed[tab[T_POS + block]]
                    if d == 0:
                        middle[ten][t, b, a_own] = piece
                    else:
                        first[ten][t, d - 1, b] = piece
        start1(OUT, t)

        @pl.when(t < KVH - 1)
        def _():
            z_send[t, 0] = (k_acc[0:VT16, :] * scale).astype(BF16)
            z_send[t, 1] = v_acc[0:VT16, :].astype(BF16)
            z_copy(t).start()

        return carry

    lax.fori_loop(0, KVH, step, 0)

    for t in range(KVH - 1):
        z_copy(t).wait_recv()

    def total_of(j, n):
        rows = pl.ds(j, n)
        sums = [k_acc[rows, :] * scale, v_acc[rows, :]]
        for t in range(KVH - 1):
            for w in (0, 1):
                sums[w] = sums[w] + z_recv[t, w, rows, :].astype(F32)
        return sums

    parts = [(j, min(256, VT16 - j)) for j in range(0, VT16, 256)]
    for j, n in parts:
        sums = total_of(j, n)
        rows = pl.ds(j, n)
        k_acc[rows, :] = sums[0]
        v_acc[rows, :] = sums[1]
        c_send[0, rows, :] = sums[0].astype(BF16)
        c_send[1, rows, :] = sums[1].astype(BF16)
    core_copy = pltpu.make_async_remote_copy(
        src_ref=c_send,
        dst_ref=c_recv,
        send_sem=cs,
        recv_sem=cw,
        device_id=(z * 2 + 1 - core, en),
        device_id_type=MESH,
    )
    core_copy.start()
    forward(OUT, KVH - 1)
    core_copy.wait_recv()
    for w, acc, out in ((0, k_acc, gk_out), (1, v_acc, gv_out)):
        for j, n in parts:
            full = acc[j : j + n, :] + c_recv[w, j : j + n, :].astype(F32)
            half = jnp.where(core == 0, full[:, 0:64], full[:, 64:128]).astype(BF16)
            if j + n > VT:
                out[0, j:1600, :] = half[0 : 1600 - j]
                out[0, 1600:VT, :] = half[1600 - j : VT - j]
            else:
                out[0, j : j + n, :] = half

    for t in range(KVH):
        arrive(OUT, t)

    def collect(t, carry):
        cols0 = head_at(t) * (GROUP * HD)
        for ten, out in ((2, att_out), (3, gq_out)):
            b_own = own[ten][1]
            for d in range(4):
                b = (b_own + d) % 4
                for a in range(4):
                    src = middle[ten] if d == 0 else last[ten]
                    stage = stage_q if ten == 2 else stage_g
                    stage[b * 4 + a] = src[t, b, a]
            for r in range(8):
                image = tab[T_READ + r]
                if ten == 2:
                    block = stage_q[(image % 4) * 4 + image // 4]
                else:
                    block = stage_g[image]
                for g in range(GROUP):
                    cols = pl.ds(pl.multiple_of(cols0 + g * HD, HD), HD)
                    out[r, :, cols] = block[g * SEG : (g + 1) * SEG, :]
        return carry

    lax.fori_loop(0, KVH, collect, 0)

    for t in range(KVH):
        for ten in range(4):
            for d in (1, 2, 3):
                hop1(ten, t, d).wait_send()
                hop2(ten, t, d).wait_send()
    for t in range(KVH - 1):
        z_copy(t).wait_send()
    core_copy.wait_send()


def tables(reads, slots):
    row = lax.axis_index("seq")
    own = lax.axis_index("enc")
    peers = 16
    row_reads = lax.dynamic_slice_in_dim(reads, row * peers, peers, 0)
    own_reads = lax.dynamic_index_in_dim(row_reads, own, 0, keepdims=False)
    ids = jnp.arange(16, dtype=jnp.int32)
    segs = jnp.arange(8, dtype=jnp.int32)
    send = jnp.sum(jnp.where(own_reads[None, :] == ids[:, None], segs[None, :], 0), axis=1)
    occupied = jnp.any(row_reads == own, axis=1)
    before = jnp.sum(
        jnp.where(occupied[None, :] & (ids[None, :] < ids[:, None]), 1, 0), axis=1
    )
    count = jnp.sum(jnp.where(occupied, 1, 0))
    place = (before[None, :] == ids[:, None]) & occupied[None, :]
    source = jnp.sum(jnp.where(place, ids[None, :], 0), axis=1)
    valid = jnp.where(ids < count, 1, 0)
    position = jnp.where(occupied, before, 0)
    return jnp.concatenate([send, source, valid, position, own_reads]).astype(jnp.int32)


def per_device(queries, keys, values, reads, grad_out):
    slots = 12
    tab = tables(reads, slots)
    q = queries.reshape(8, SEG, HQ * HD)
    g = grad_out.reshape(8, SEG, HQ * HD)
    whole = pl.BlockSpec(memory_space=pltpu.VMEM)
    unit = (ROWS, HD)
    out = pl.pallas_call(
        functools.partial(kernel, slots),
        out_shape=(
            jax.ShapeDtypeStruct(q.shape, BF16),
            jax.ShapeDtypeStruct(q.shape, BF16),
            jax.ShapeDtypeStruct((1, VT, 64), BF16),
            jax.ShapeDtypeStruct((1, VT, 64), BF16),
        ),
        in_specs=[pl.BlockSpec(memory_space=pltpu.SMEM)] + [whole] * 4,
        out_specs=(whole,) * 4,
        scratch_shapes=[pltpu.VMEM((KVH, 3, 4) + unit, BF16)] * 4
        + [pltpu.VMEM((KVH, 4, 4) + unit, BF16)] * 8
        + [pltpu.VMEM((KVH, JP, HD), BF16)] * 2
        + [pltpu.VMEM((KVH, HD, JP), BF16)] * 2
        + [pltpu.VMEM((16,) + unit, BF16)] * 2
        + [pltpu.VMEM((slots,) + unit, BF16)] * 2
        + [
            pltpu.VMEM((JP, 2 * ROWS), F32),
            pltpu.VMEM((JP, 2 * ROWS), BF16),
            pltpu.VMEM((JP, HD), F32),
            pltpu.VMEM((JP, HD), F32),
            pltpu.VMEM((KVH - 1, 2, VT16, HD), BF16),
            pltpu.VMEM((KVH - 1, 2, VT16, HD), BF16),
            pltpu.VMEM((2, VT16, HD), BF16),
            pltpu.VMEM((2, VT16, HD), BF16),
        ]
        + [pltpu.SemaphoreType.DMA((4, KVH, 3))] * 4
        + [pltpu.SemaphoreType.DMA((KVH - 1,))] * 2
        + [pltpu.SemaphoreType.DMA] * 2,
        compiler_params=pltpu.CompilerParams(
            collective_id=0, has_side_effects=True, vmem_limit_bytes=60 * 1024 * 1024
        ),
    )(tab, q, g, keys, values)
    attended, grad_queries, grad_keys, grad_values = out
    return (
        attended.reshape(queries.shape),
        grad_queries.reshape(queries.shape),
        grad_keys,
        grad_values,
    )


def solution(mesh):
    placed = (
        P(("seq", "enc"), None),
        P("enc", None, None),
        P("enc", None, None),
        P(),
        P(("seq", "enc"), None),
    )
    return jax.shard_map(
        per_device,
        mesh=mesh,
        in_specs=placed,
        out_specs=(
            P(("seq", "enc"), None),
            P(("seq", "enc"), None),
            P("enc", None, "seq"),
            P("enc", None, "seq"),
        ),
        check_vma=False,
    )
```

```python
import functools

import jax
import jax.numpy as jnp
from jax import lax
from jax.experimental import pallas as pl
from jax.experimental.pallas import tpu as pltpu
from jax.sharding import PartitionSpec as P

HQ = 32
KVH = 4
HD = 128
HALF = HQ // KVH // 2
SEG = 16
ROWS = HALF * SEG
STEPS = 2 * KVH
SLOTS = 12
WIDE = SLOTS * ROWS
VT = 1601
VT16 = 1616
JP = 1664
LOG2E = 1.4426950408889634
MESH = pl.DeviceIdType.MESH
BF16 = jnp.bfloat16
F32 = jnp.float32
CHUNKS = [(j, min(256, JP - j)) for j in range(0, JP, 256)]
NT = (((1,), (1,)), ((), ()))
IN, OUT = (0, 1), (2, 3)
AHEAD = 4
T_SEND, T_SRC, T_OK, T_POS = 0, 16, 32, 48


def kernel(
    reads, q_hbm, g_hbm, k_hbm, v_hbm, att_out, gq_out, gk_out, gv_out,
    tab, q_in, g_in, k_in, v_in, att_v, gq_v,
    a_q, a_g, a_o, a_d, m_q, m_g, m_o, m_d, r_q, r_g, r_o, r_d,
    kh, vh, kt, vt, stage_q, stage_g, pack_o, pack_d, s_scr, p_scr, k_acc, v_acc,
    z_send, z_recv, c_send, c_recv,
    s1, w1, s2, w2, zs, zw, cs, cw, ls, lo, lk,
):
    sq = lax.axis_index("seq")
    en = lax.axis_index("enc")
    z, core = sq // 2, sq % 2
    x, y = en // 4, en % 4
    scale = HD ** (-0.5)

    first = (a_q, a_g, a_o, a_d)
    middle = (m_q, m_g, m_o, m_d)
    last = (r_q, r_g, r_o, r_d)
    own = [(x, y), (y, x), (x, y), (y, x)]

    def peer(axis, d):
        if axis == 0:
            return (sq, ((x + d) % 4) * 4 + y)
        return (sq, x * 4 + (y + d) % 4)

    def hop1(ten, s, d):
        return pltpu.make_async_remote_copy(
            src_ref=first[ten].at[s, d - 1],
            dst_ref=middle[ten].at[s, :, own[ten][0]],
            send_sem=s1.at[ten, s, d - 1],
            recv_sem=w1.at[ten, s, d - 1],
            device_id=peer(ten % 2, d),
            device_id_type=MESH,
        )

    def hop2(ten, s, d):
        b = own[ten][1]
        return pltpu.make_async_remote_copy(
            src_ref=middle[ten].at[s, (b + d) % 4],
            dst_ref=last[ten].at[s, b],
            send_sem=s2.at[ten, s, d - 1],
            recv_sem=w2.at[ten, s, d - 1],
            device_id=peer(1 - ten % 2, d),
            device_id_type=MESH,
        )

    def start1(pair, s):
        for d in (2, 1, 3):
            for ten in pair:
                hop1(ten, s, d).start()

    def forward(pair, s):
        for ten in pair:
            for d in (1, 2, 3):
                hop1(ten, s, d).wait_recv()
            for d in (2, 1, 3):
                hop2(ten, s, d).start()

    def arrive(pair, s):
        for ten in pair:
            for d in (1, 2, 3):
                hop2(ten, s, d).wait_recv()

    def sent(pair, s):
        for ten in pair:
            for d in (1, 2, 3):
                hop1(ten, s, d).wait_send()
                hop2(ten, s, d).wait_send()

    def head_at(t):
        return (z + 1 + t) % 4

    def z_copy(t):
        return pltpu.make_async_remote_copy(
            src_ref=z_send.at[t],
            dst_ref=z_recv.at[t],
            send_sem=zs.at[t],
            recv_sem=zw.at[t],
            device_id=(head_at(t) * 2 + core, en),
            device_id_type=MESH,
        )

    def load(ten, t):
        cols = pl.ds(pl.multiple_of(head_at(t) * (2 * HALF * HD), 2 * HALF * HD), 2 * HALF * HD)
        src, dst = ((q_hbm, q_in), (g_hbm, g_in))[ten]
        return pltpu.make_async_copy(src.at[:, :, cols], dst.at[t], ls.at[ten, t])

    barrier = pltpu.get_barrier_semaphore()
    for d in (1, 2, 3):
        for target in (peer(0, d), peer(1, d), (((z + d) % 4) * 2 + core, en)):
            pl.semaphore_signal(barrier, inc=1, device_id=target, device_id_type=MESH)
    pl.semaphore_signal(barrier, inc=1, device_id=(z * 2 + 1 - core, en), device_id_type=MESH)
    for t in range(KVH):
        load(0, t).start()
        load(1, t).start()
    loads_kv = [
        pltpu.make_async_copy(k_hbm.at[0], k_in, lk.at[0]),
        pltpu.make_async_copy(v_hbm.at[0], v_in, lk.at[1]),
    ]
    for copy in loads_kv:
        copy.start()

    block_row = sq * 16 + en
    own_reads = [reads[r, block_row] for r in range(8)]
    for image in range(16):
        found = jnp.int32(0)
        for r in range(1, 8):
            found = jnp.where(own_reads[r] == image, r, found)
        tab[T_SEND + image] = found

    def pack_in(s):
        t, u = s // 2, s % 2
        cols = pl.ds(pl.multiple_of(u * (HALF * HD), HALF * HD), HALF * HD)
        for ten, src in ((0, q_in), (1, g_in)):
            a_own = own[ten][0]
            for d in range(4):
                a = (a_own + d) % 4
                for b in range(4):
                    image = a * 4 + b if ten == 0 else b * 4 + a
                    block = src[t, tab[T_SEND + image], :, cols]
                    for g in range(HALF):
                        piece = block[:, g * HD : (g + 1) * HD]
                        rows = pl.ds(g * SEG, SEG)
                        if d == 0:
                            middle[ten][s, b, a_own, rows, :] = piece
                        else:
                            first[ten][s, d - 1, b, rows, :] = piece

    for t in range(KVH):
        load(0, t).wait()
        load(1, t).wait()
    pack_in(jnp.int32(0))
    pl.semaphore_wait(barrier, 10)
    start1(IN, 0)

    def send_in(s, carry):
        pack_in(s)

        @pl.when(s < AHEAD)
        def _():
            start1(IN, s)

        return carry

    lax.fori_loop(1, STEPS, send_in, 0)

    count = jnp.int32(0)
    places = []
    for b in range(16):
        named = reads[0, sq * 16 + b] == en
        for r in range(1, 8):
            named = named | (reads[r, sq * 16 + b] == en)
        flag = jnp.where(named, 1, 0)
        tab[T_POS + b] = jnp.where(named, jnp.minimum(count, SLOTS - 1), 0)
        places.append(jnp.where(named, count, -1))
        count = count + flag
    for m in range(SLOTS):
        source = jnp.int32(0)
        for b in range(16):
            source = jnp.where(places[b] == m, b, source)
        tab[T_SRC + m] = source
        tab[T_OK + m] = jnp.where(count > m, 1, 0)

    forward(IN, 0)
    start1(IN, AHEAD)

    for copy in loads_kv:
        copy.wait()

    def heads(t, carry):
        cols = pl.ds(pl.multiple_of(head_at(t) * HD, HD), HD)
        for src, rows_ref, cols_ref in ((k_in, kh, kt), (v_in, vh, vt)):
            rows_ref[t, 0:1600, :] = src[0:1600, cols]
            tail = src[1600:VT, cols].astype(F32)
            mark = lax.broadcasted_iota(jnp.int32, (64, HD), 0) == 0
            rows_ref[t, 1600:JP, :] = jnp.where(
                mark, jnp.broadcast_to(tail, (64, HD)), 0.0
            ).astype(BF16)
            for j in range(0, JP, HD):
                cols_ref[t, :, j : j + HD] = rows_ref[t, j : j + HD, :].T
        return carry

    lax.fori_loop(0, 2, heads, 0)
    forward(IN, 1)
    start1(IN, AHEAD + 1)
    lax.fori_loop(2, KVH, heads, 0)
    forward(IN, 2)
    start1(IN, AHEAD + 2)

    def step(s, carry):
        t, u = s // 2, s % 2
        arrive(IN, s)
        for ten, stage in ((0, stage_q), (1, stage_g)):
            b_own = own[ten][1]
            for d in range(4):
                b = (b_own + d) % 4
                for a in range(4):
                    if d == 0:
                        stage[b * 4 + a] = middle[ten][s, b, a]
                    else:
                        stage[b * 4 + a] = last[ten][s, b, a]

        @pl.when(s + 3 < STEPS)
        def _():
            forward(IN, s + 3)

        @pl.when(s + 3 + AHEAD < STEPS)
        def _():
            start1(IN, s + 3 + AHEAD)

        @pl.when(u == 0)
        def _():
            k_acc[...] = jnp.zeros_like(k_acc)
            v_acc[...] = jnp.zeros_like(v_acc)

        q_parts, g_parts = [], []
        for m in range(SLOTS):
            source = tab[T_SRC + m]
            q_parts.append(stage_q[(source % 4) * 4 + source // 4])
            g_parts.append(jnp.where(tab[T_OK + m] > 0, stage_g[source].astype(F32), 0.0))
        q = jnp.concatenate(q_parts, axis=0)
        g_t = jnp.concatenate(g_parts, axis=0).T

        top = jnp.full((8, WIDE), -jnp.inf, F32)
        for j, n in CHUNKS:
            sc = lax.dot_general(kh[t, j : j + n, :], q, NT, preferred_element_type=F32)
            if j + n > VT:
                row = lax.broadcasted_iota(jnp.int32, sc.shape, 0) + j
                sc = jnp.where(row < VT, sc, -1e30)
            s_scr[j : j + n, :] = sc
            top = jnp.maximum(top, jnp.max(sc.reshape(n // 8, 8, WIDE), axis=0))
        c2 = scale * LOG2E
        top2 = jnp.max(top, axis=0, keepdims=True) * c2
        total = jnp.zeros((8, WIDE), F32)
        o_t = jnp.zeros((HD, WIDE), F32)
        for j, n in CHUNKS:
            p = jnp.exp2(s_scr[j : j + n, :] * c2 - top2)
            total += jnp.sum(p.reshape(n // 8, 8, WIDE), axis=0)
            p_b = p.astype(BF16)
            p_scr[j : j + n, :] = p_b
            o_t += jnp.dot(vt[t, :, j : j + n], p_b, preferred_element_type=F32)
        inv = 1.0 / jnp.sum(total, axis=0, keepdims=True)
        o_t = (o_t * inv).astype(BF16).astype(F32)
        pack_o[...] = o_t.T.astype(BF16).reshape(SLOTS, ROWS, HD)

        @pl.when(s > 1)
        def _():
            forward(OUT, s - 2)

        delta = jnp.sum(g_t * o_t, axis=0, keepdims=True) * inv
        g_s = (g_t * inv).astype(BF16)
        d_t = jnp.zeros((HD, WIDE), F32)
        for j, n in CHUNKS:
            dp = jnp.dot(vh[t, j : j + n, :], g_s, preferred_element_type=F32)
            p_b = p_scr[j : j + n, :]
            ds = (p_b.astype(F32) * (dp - delta)).astype(BF16)
            v_acc[j : j + n, :] += lax.dot_general(p_b, g_s, NT, preferred_element_type=F32)
            k_acc[j : j + n, :] += jnp.dot(ds, q, preferred_element_type=F32)
            d_t += jnp.dot(kt[t, :, j : j + n], ds, preferred_element_type=F32)
        pack_d[...] = (d_t * scale).T.astype(BF16).reshape(SLOTS, ROWS, HD)

        for ten, packed in ((2, pack_o), (3, pack_d)):
            a_own = own[ten][0]
            for d in range(4):
                a = (a_own + d) % 4
                for b in range(4):
                    block = a * 4 + b if ten == 2 else b * 4 + a
                    piece = packed[tab[T_POS + block]]
                    if d == 0:
                        middle[ten][s, b, a_own] = piece
                    else:
                        first[ten][s, d - 1, b] = piece
        start1(OUT, s)

        @pl.when((u == 1) & (t < KVH - 1))
        def _():
            z_send[t, 0] = (k_acc[0:VT16, :] * scale).astype(BF16)
            z_send[t, 1] = v_acc[0:VT16, :].astype(BF16)
            z_copy(t).start()

        return carry

    lax.fori_loop(0, STEPS, step, 0)

    parts = [(j, min(256, VT16 - j)) for j in range(0, VT16, 256)]
    for t in range(KVH - 1):
        z_copy(t).wait_recv()
    forward(OUT, STEPS - 2)
    for j, n in parts:
        rows = pl.ds(j, n)
        sums = [k_acc[rows, :] * scale, v_acc[rows, :]]
        for w, acc in ((0, k_acc), (1, v_acc)):
            for t in range(KVH - 1):
                sums[w] = sums[w] + z_recv[t, w, rows, :].astype(F32)
            acc[rows, :] = sums[w]
            c_send[w, rows, :] = sums[w].astype(BF16)
    core_copy = pltpu.make_async_remote_copy(
        src_ref=c_send,
        dst_ref=c_recv,
        send_sem=cs,
        recv_sem=cw,
        device_id=(z * 2 + 1 - core, en),
        device_id_type=MESH,
    )
    core_copy.start()
    forward(OUT, STEPS - 1)

    def out_copy(ten, s):
        cols = pl.ds(
            pl.multiple_of((head_at(s // 2) * 2 + s % 2) * (HALF * HD), HALF * HD), HALF * HD
        )
        src, dst = ((att_v, att_out), (gq_v, gq_out))[ten - 2]
        return pltpu.make_async_copy(src.at[s], dst.at[:, :, cols], lo.at[ten - 2, s])

    def collect(s, carry):
        arrive(OUT, s)
        for ten, stage, out in ((2, stage_q, att_v), (3, stage_g, gq_v)):
            b_own = own[ten][1]
            for d in range(4):
                b = (b_own + d) % 4
                for a in range(4):
                    src = middle[ten] if d == 0 else last[ten]
                    stage[b * 4 + a] = src[s, b, a]
            for r in range(8):
                image = reads[r, block_row]
                if ten == 2:
                    block = stage[(image % 4) * 4 + image // 4]
                else:
                    block = stage[image]
                for g in range(HALF):
                    out[s, r, :, g * HD : (g + 1) * HD] = block[g * SEG : (g + 1) * SEG, :]
            out_copy(ten, s).start()
        return carry

    def finish(s, carry):
        sent(IN, s)
        sent(OUT, s)
        out_copy(2, s).wait()
        out_copy(3, s).wait()
        return carry

    lax.fori_loop(0, STEPS - 2, collect, 0)
    core_copy.wait_recv()
    for w, acc, out in ((0, k_acc, gk_out), (1, v_acc, gv_out)):
        for j in range(0, VT, HD):
            n = min(HD, VT16 - j)
            full = acc[j : j + n, :] + c_recv[w, j : j + n, :].astype(F32)
            if n < HD:
                full = jnp.concatenate([full, jnp.zeros((HD - n, HD), F32)], axis=0)
            turned = full.T
            half = jnp.where(core == 0, turned[0:64], turned[64:128]).astype(BF16)
            if j + HD > VT:
                out[0, :, j:VT] = half[:, 0 : VT - j]
            else:
                out[0, :, j : j + HD] = half
    lax.fori_loop(0, STEPS - 2, finish, 0)
    for t in range(KVH - 1):
        z_copy(t).wait_send()
    core_copy.wait_send()
    lax.fori_loop(STEPS - 2, STEPS, collect, 0)
    lax.fori_loop(STEPS - 2, STEPS, finish, 0)


def per_device(queries, keys, values, reads, grad_out):
    q = queries.reshape(8, SEG, HQ * HD)
    g = grad_out.reshape(8, SEG, HQ * HD)
    vmem = pl.BlockSpec(memory_space=pltpu.VMEM)
    hbm = pl.BlockSpec(memory_space=pl.ANY)
    unit = (ROWS, HD)
    attended, grad_queries, grad_keys, grad_values = pl.pallas_call(
        kernel,
        out_shape=(
            jax.ShapeDtypeStruct(q.shape, BF16),
            jax.ShapeDtypeStruct(q.shape, BF16),
            jax.ShapeDtypeStruct((1, 64, VT), BF16),
            jax.ShapeDtypeStruct((1, 64, VT), BF16),
        ),
        in_specs=[pl.BlockSpec(memory_space=pltpu.SMEM)] + [hbm] * 4,
        out_specs=(hbm, hbm, vmem, vmem),
        scratch_shapes=[pltpu.SMEM((64,), jnp.int32)]
        + [pltpu.VMEM((KVH, 8, SEG, 2 * HALF * HD), BF16)] * 2
        + [pltpu.VMEM((VT, KVH * HD), BF16)] * 2
        + [pltpu.VMEM((STEPS, 8, SEG, HALF * HD), BF16)] * 2
        + [pltpu.VMEM((STEPS, 3, 4) + unit, BF16)] * 4
        + [pltpu.VMEM((STEPS, 4, 4) + unit, BF16)] * 8
        + [pltpu.VMEM((KVH, JP, HD), BF16)] * 2
        + [pltpu.VMEM((KVH, HD, JP), BF16)] * 2
        + [pltpu.VMEM((16,) + unit, BF16)] * 2
        + [pltpu.VMEM((SLOTS,) + unit, BF16)] * 2
        + [
            pltpu.VMEM((JP, WIDE), F32),
            pltpu.VMEM((JP, WIDE), BF16),
            pltpu.VMEM((JP, HD), F32),
            pltpu.VMEM((JP, HD), F32),
            pltpu.VMEM((KVH - 1, 2, VT16, HD), BF16),
            pltpu.VMEM((KVH - 1, 2, VT16, HD), BF16),
            pltpu.VMEM((2, VT16, HD), BF16),
            pltpu.VMEM((2, VT16, HD), BF16),
        ]
        + [pltpu.SemaphoreType.DMA((4, STEPS, 3))] * 4
        + [pltpu.SemaphoreType.DMA((KVH - 1,))] * 2
        + [pltpu.SemaphoreType.DMA] * 2
        + [
            pltpu.SemaphoreType.DMA((2, KVH)),
            pltpu.SemaphoreType.DMA((2, STEPS)),
            pltpu.SemaphoreType.DMA((2,)),
        ],
        compiler_params=pltpu.CompilerParams(
            collective_id=0, has_side_effects=True, vmem_limit_bytes=62 * 1024 * 1024
        ),
    )(reads.T, q, g, keys, values)
    return (
        attended.reshape(queries.shape),
        grad_queries.reshape(queries.shape),
        jnp.swapaxes(grad_keys, 1, 2),
        jnp.swapaxes(grad_values, 1, 2),
    )


def solution(mesh):
    placed = (
        P(("seq", "enc"), None),
        P("enc", None, None),
        P("enc", None, None),
        P(),
        P(("seq", "enc"), None),
    )
    return jax.shard_map(
        per_device,
        mesh=mesh,
        in_specs=placed,
        out_specs=(
            P(("seq", "enc"), None),
            P(("seq", "enc"), None),
            P("enc", None, "seq"),
            P("enc", None, "seq"),
        ),
        check_vma=False,
    )
```

```python
import functools

import jax
import jax.numpy as jnp
from jax import lax
from jax.experimental import pallas as pl
from jax.experimental.pallas import tpu as pltpu
from jax.sharding import PartitionSpec as P

HQ = 32
KVH = 4
HD = 128
HALF = HQ // KVH // 2
SEG = 16
ROWS = HALF * SEG
STEPS = 2 * KVH
SLOTS = 12
WIDE = SLOTS * ROWS
VT = 1601
VT16 = 1616
JP = 1664
LOG2E = 1.4426950408889634
MESH = pl.DeviceIdType.MESH
BF16 = jnp.bfloat16
F32 = jnp.float32
CHUNKS = [(j, min(256, JP - j)) for j in range(0, JP, 256)]
NT = (((1,), (1,)), ((), ()))
IN, OUT = (0, 1), (2, 3)
AHEAD = 4
T_SEND, T_SRC, T_OK, T_POS = 0, 16, 32, 48


def kernel(
    reads, q_hbm, g_hbm, k_hbm, v_hbm, att_out, gq_out, gk_out, gv_out,
    tab, q_0, g_0, q_in, g_in, k_in, v_in, att_v, gq_v,
    a_q, a_g, a_o, a_d, m_q, m_g, m_o, m_d, r_q, r_g, r_o, r_d,
    kh, vh, kt, vt, stage_q, stage_g, pack_o, pack_d, s_scr, p_scr, k_acc, v_acc,
    z_send, z_recv, c_send, c_recv,
    s1, w1, s2, w2, zs, zw, cs, cw, l0, ls, lo, lk,
):
    sq = lax.axis_index("seq")
    en = lax.axis_index("enc")
    z, core = sq // 2, sq % 2
    x, y = en // 4, en % 4
    scale = HD ** (-0.5)

    first = (a_q, a_g, a_o, a_d)
    middle = (m_q, m_g, m_o, m_d)
    last = (r_q, r_g, r_o, r_d)
    own = [(x, y), (y, x), (x, y), (y, x)]

    def peer(axis, d):
        if axis == 0:
            return (sq, ((x + d) % 4) * 4 + y)
        return (sq, x * 4 + (y + d) % 4)

    def hop1(ten, s, d):
        return pltpu.make_async_remote_copy(
            src_ref=first[ten].at[s, d - 1],
            dst_ref=middle[ten].at[s, :, own[ten][0]],
            send_sem=s1.at[ten],
            recv_sem=w1.at[ten, s],
            device_id=peer(ten % 2, d),
            device_id_type=MESH,
        )

    def hop2(ten, s, d):
        b = own[ten][1]
        return pltpu.make_async_remote_copy(
            src_ref=middle[ten].at[s, (b + d) % 4],
            dst_ref=last[ten].at[s, b],
            send_sem=s2.at[ten],
            recv_sem=w2.at[ten // 2, s],
            device_id=peer(1 - ten % 2, d),
            device_id_type=MESH,
        )

    def start1(pair, s):
        for d in (2, 1, 3):
            for ten in pair:
                hop1(ten, s, d).start()

    def await_recv(ref, sem):
        pltpu.make_async_remote_copy(
            src_ref=ref, dst_ref=ref, send_sem=s1.at[0], recv_sem=sem,
            device_id=peer(0, 1), device_id_type=MESH,
        ).wait_recv()

    def await_send(ref, sem):
        pltpu.make_async_remote_copy(
            src_ref=ref, dst_ref=ref, send_sem=sem, recv_sem=w1.at[0, 0],
            device_id=peer(0, 1), device_id_type=MESH,
        ).wait_send()

    def forward(pair, s):
        for ten in pair:
            await_recv(first[ten].at[s], w1.at[ten, s])
            for d in (2, 1, 3):
                hop2(ten, s, d).start()

    def arrive(pair, s):
        await_recv(first[pair[0]].at[pl.ds(0, 2)], w2.at[pair[0] // 2, s])

    def head_at(t):
        return (z + 1 + t) % 4

    def z_copy(t):
        return pltpu.make_async_remote_copy(
            src_ref=z_send.at[t],
            dst_ref=z_recv.at[t],
            send_sem=zs.at[t],
            recv_sem=zw.at[t],
            device_id=(head_at(t) * 2 + core, en),
            device_id_type=MESH,
        )

    def load(ten, t):
        cols = pl.ds(pl.multiple_of(head_at(t) * (2 * HALF * HD), 2 * HALF * HD), 2 * HALF * HD)
        src, dst = ((q_hbm, q_in), (g_hbm, g_in))[ten]
        if t == 0:
            return pltpu.make_async_copy(src.at[:, :, cols], (q_0, g_0)[ten], l0.at[ten])
        return pltpu.make_async_copy(src.at[:, :, cols], dst.at[t - 1], ls.at[ten])

    barrier = pltpu.get_barrier_semaphore()
    for d in (1, 2, 3):
        for target in (peer(0, d), peer(1, d), (((z + d) % 4) * 2 + core, en)):
            pl.semaphore_signal(barrier, inc=1, device_id=target, device_id_type=MESH)
    pl.semaphore_signal(barrier, inc=1, device_id=(z * 2 + 1 - core, en), device_id_type=MESH)
    for t in range(KVH):
        load(0, t).start()
        load(1, t).start()
    loads_kv = [
        pltpu.make_async_copy(k_hbm.at[0], k_in, lk.at[0]),
        pltpu.make_async_copy(v_hbm.at[0], v_in, lk.at[1]),
    ]
    for copy in loads_kv:
        copy.start()

    block_row = sq * 16 + en
    own_reads = [reads[r, block_row] for r in range(8)]
    for image in range(16):
        found = jnp.int32(0)
        for r in range(1, 8):
            found = jnp.where(own_reads[r] == image, r, found)
        tab[T_SEND + image] = found

    def pack_in(s, u, sources):
        cols = pl.ds(pl.multiple_of(u * (HALF * HD), HALF * HD), HALF * HD)
        for ten, src in ((0, sources[0]), (1, sources[1])):
            a_own = own[ten][0]
            for d in range(4):
                a = (a_own + d) % 4
                for b in range(4):
                    image = a * 4 + b if ten == 0 else b * 4 + a
                    block = src[tab[T_SEND + image], :, cols]
                    for g in range(HALF):
                        piece = block[:, g * HD : (g + 1) * HD]
                        rows = pl.ds(g * SEG, SEG)
                        if d == 0:
                            middle[ten][s, b, a_own, rows, :] = piece
                        else:
                            first[ten][s, d - 1, b, rows, :] = piece

    load(0, 0).wait()
    load(1, 0).wait()
    pack_in(0, 0, (q_0, g_0))
    pl.semaphore_wait(barrier, 10)
    start1(IN, 0)
    pack_in(1, 1, (q_0, g_0))
    start1(IN, 1)
    pltpu.make_async_copy(q_in, q_in, ls.at[0]).wait()
    pltpu.make_async_copy(g_in, g_in, ls.at[1]).wait()

    def send_in(s, carry):
        pack_in(s, s % 2, (q_in.at[s // 2 - 1], g_in.at[s // 2 - 1]))

        @pl.when(s < AHEAD)
        def _():
            start1(IN, s)

        return carry

    lax.fori_loop(2, STEPS, send_in, 0)

    count = jnp.int32(0)
    places = []
    for b in range(16):
        named = reads[0, sq * 16 + b] == en
        for r in range(1, 8):
            named = named | (reads[r, sq * 16 + b] == en)
        flag = jnp.where(named, 1, 0)
        tab[T_POS + b] = jnp.where(named, jnp.minimum(count, SLOTS - 1), 0)
        places.append(jnp.where(named, count, -1))
        count = count + flag
    for m in range(SLOTS):
        source = jnp.int32(0)
        for b in range(16):
            source = jnp.where(places[b] == m, b, source)
        tab[T_SRC + m] = source
        tab[T_OK + m] = jnp.where(count > m, 1, 0)

    forward(IN, 0)
    start1(IN, AHEAD)

    for copy in loads_kv:
        copy.wait()

    def heads(t, carry):
        cols = pl.ds(pl.multiple_of(head_at(t) * HD, HD), HD)
        for src, rows_ref, cols_ref in ((k_in, kh, kt), (v_in, vh, vt)):
            rows_ref[t, 0:1600, :] = src[0:1600, cols]
            tail = src[1600:VT, cols].astype(F32)
            mark = lax.broadcasted_iota(jnp.int32, (64, HD), 0) == 0
            rows_ref[t, 1600:JP, :] = jnp.where(
                mark, jnp.broadcast_to(tail, (64, HD)), 0.0
            ).astype(BF16)
            for j in range(0, JP, HD):
                cols_ref[t, :, j : j + HD] = rows_ref[t, j : j + HD, :].T
        return carry

    lax.fori_loop(0, 2, heads, 0)
    forward(IN, 1)
    start1(IN, AHEAD + 1)
    lax.fori_loop(2, KVH, heads, 0)
    forward(IN, 2)
    start1(IN, AHEAD + 2)

    def step(s, carry):
        t, u = s // 2, s % 2
        arrive(IN, s)
        for ten, stage in ((0, stage_q), (1, stage_g)):
            b_own = own[ten][1]
            for d in range(4):
                b = (b_own + d) % 4
                for a in range(4):
                    if d == 0:
                        stage[b * 4 + a] = middle[ten][s, b, a]
                    else:
                        stage[b * 4 + a] = last[ten][s, b, a]

        @pl.when(s + 3 < STEPS)
        def _():
            forward(IN, s + 3)

        @pl.when(s + 3 + AHEAD < STEPS)
        def _():
            start1(IN, s + 3 + AHEAD)

        @pl.when(u == 0)
        def _():
            k_acc[...] = jnp.zeros_like(k_acc)
            v_acc[...] = jnp.zeros_like(v_acc)

        q_parts, g_parts = [], []
        for m in range(SLOTS):
            source = tab[T_SRC + m]
            q_parts.append(stage_q[(source % 4) * 4 + source // 4])
            g_parts.append(jnp.where(tab[T_OK + m] > 0, stage_g[source].astype(F32), 0.0))
        q = jnp.concatenate(q_parts, axis=0)
        g_t = jnp.concatenate(g_parts, axis=0).T

        top = jnp.full((8, WIDE), -jnp.inf, F32)
        for j, n in CHUNKS:
            sc = lax.dot_general(kh[t, j : j + n, :], q, NT, preferred_element_type=F32)
            if j + n > VT:
                row = lax.broadcasted_iota(jnp.int32, sc.shape, 0) + j
                sc = jnp.where(row < VT, sc, -1e30)
            s_scr[j : j + n, :] = sc
            top = jnp.maximum(top, jnp.max(sc.reshape(n // 8, 8, WIDE), axis=0))
        c2 = scale * LOG2E
        top2 = jnp.max(top, axis=0, keepdims=True) * c2
        total = jnp.zeros((8, WIDE), F32)
        o_t = jnp.zeros((HD, WIDE), F32)
        for j, n in CHUNKS:
            p = jnp.exp2(s_scr[j : j + n, :] * c2 - top2)
            total += jnp.sum(p.reshape(n // 8, 8, WIDE), axis=0)
            p_b = p.astype(BF16)
            p_scr[j : j + n, :] = p_b
            o_t += jnp.dot(vt[t, :, j : j + n], p_b, preferred_element_type=F32)
        inv = 1.0 / jnp.sum(total, axis=0, keepdims=True)
        o_t = (o_t * inv).astype(BF16).astype(F32)
        pack_o[...] = o_t.T.astype(BF16).reshape(SLOTS, ROWS, HD)

        @pl.when(s > 1)
        def _():
            forward(OUT, s - 2)

        delta = jnp.sum(g_t * o_t, axis=0, keepdims=True) * inv
        g_s = (g_t * inv).astype(BF16)
        d_t = jnp.zeros((HD, WIDE), F32)
        for j, n in CHUNKS:
            dp = jnp.dot(vh[t, j : j + n, :], g_s, preferred_element_type=F32)
            p_b = p_scr[j : j + n, :]
            ds = (p_b.astype(F32) * (dp - delta)).astype(BF16)
            v_acc[j : j + n, :] += lax.dot_general(p_b, g_s, NT, preferred_element_type=F32)
            k_acc[j : j + n, :] += jnp.dot(ds, q, preferred_element_type=F32)
            d_t += jnp.dot(kt[t, :, j : j + n], ds, preferred_element_type=F32)
        pack_d[...] = (d_t * scale).T.astype(BF16).reshape(SLOTS, ROWS, HD)

        for ten, packed in ((2, pack_o), (3, pack_d)):
            a_own = own[ten][0]
            for d in range(4):
                a = (a_own + d) % 4
                for b in range(4):
                    block = a * 4 + b if ten == 2 else b * 4 + a
                    piece = packed[tab[T_POS + block]]
                    if d == 0:
                        middle[ten][s, b, a_own] = piece
                    else:
                        first[ten][s, d - 1, b] = piece
        start1(OUT, s)

        @pl.when((u == 1) & (t < KVH - 1))
        def _():
            z_send[t, 0] = (k_acc[0:VT16, :] * scale).astype(BF16)
            z_send[t, 1] = v_acc[0:VT16, :].astype(BF16)
            z_copy(t).start()

        return carry

    lax.fori_loop(0, STEPS, step, 0)

    parts = [(j, min(256, VT16 - j)) for j in range(0, VT16, 256)]
    for t in range(KVH - 1):
        z_copy(t).wait_recv()
    forward(OUT, STEPS - 2)
    for j, n in parts:
        rows = pl.ds(j, n)
        sums = [k_acc[rows, :] * scale, v_acc[rows, :]]
        for w, acc in ((0, k_acc), (1, v_acc)):
            for t in range(KVH - 1):
                sums[w] = sums[w] + z_recv[t, w, rows, :].astype(F32)
            acc[rows, :] = sums[w]
            c_send[w, rows, :] = sums[w].astype(BF16)
    core_copy = pltpu.make_async_remote_copy(
        src_ref=c_send,
        dst_ref=c_recv,
        send_sem=cs,
        recv_sem=cw,
        device_id=(z * 2 + 1 - core, en),
        device_id_type=MESH,
    )
    core_copy.start()
    forward(OUT, STEPS - 1)

    def out_copy(ten, s):
        cols = pl.ds(
            pl.multiple_of((head_at(s // 2) * 2 + s % 2) * (HALF * HD), HALF * HD), HALF * HD
        )
        src, dst = ((att_v, att_out), (gq_v, gq_out))[ten - 2]
        return pltpu.make_async_copy(src.at[s], dst.at[:, :, cols], lo.at[ten - 2])

    def collect(s, carry):
        arrive(OUT, s)
        for ten, stage, out in ((2, stage_q, att_v), (3, stage_g, gq_v)):
            b_own = own[ten][1]
            for d in range(4):
                b = (b_own + d) % 4
                for a in range(4):
                    src = middle[ten] if d == 0 else last[ten]
                    stage[b * 4 + a] = src[s, b, a]
            for r in range(8):
                image = reads[r, block_row]
                if ten == 2:
                    block = stage[(image % 4) * 4 + image // 4]
                else:
                    block = stage[image]
                for g in range(HALF):
                    out[s, r, :, g * HD : (g + 1) * HD] = block[g * SEG : (g + 1) * SEG, :]
            out_copy(ten, s).start()
        return carry

    lax.fori_loop(0, STEPS - 2, collect, 0)
    core_copy.wait_recv()
    for w, acc, out in ((0, k_acc, gk_out), (1, v_acc, gv_out)):
        for j in range(0, VT, HD):
            n = min(HD, VT16 - j)
            full = acc[j : j + n, :] + c_recv[w, j : j + n, :].astype(F32)
            if n < HD:
                full = jnp.concatenate([full, jnp.zeros((HD - n, HD), F32)], axis=0)
            turned = full.T
            half = jnp.where(core == 0, turned[0:64], turned[64:128]).astype(BF16)
            if j + HD > VT:
                out[0, :, j:VT] = half[:, 0 : VT - j]
            else:
                out[0, :, j : j + HD] = half
    for t in range(KVH - 1):
        z_copy(t).wait_send()
    core_copy.wait_send()
    lax.fori_loop(STEPS - 2, STEPS, collect, 0)
    for ten in range(4):
        await_send(first[ten], s1.at[ten])
        await_send(first[ten], s2.at[ten])
    pltpu.make_async_copy(att_v, att_v, lo.at[0]).wait()
    pltpu.make_async_copy(gq_v, gq_v, lo.at[1]).wait()


def copy_out(*refs):
    sources, targets, buffers, sems = refs[0:4], refs[4:8], refs[8:12], refs[12]
    copies = []
    for i in range(4):
        rows = sources[i].shape[0]
        for p in range(2 if rows > 1 else 1):
            part = pl.ds(p * (rows // 2), rows // 2) if rows > 1 else pl.ds(0, 1)
            into = pltpu.make_async_copy(
                sources[i].at[part], buffers[i].at[part], sems.at[0, i, p]
            )
            into.start()
            copies.append(
                (into, pltpu.make_async_copy(buffers[i].at[part], targets[i].at[part], sems.at[1, i, p]))
            )
    for into, back in copies:
        into.wait()
        back.start()
    for into, back in copies:
        back.wait()


def per_device(queries, keys, values, reads, grad_out):
    q = queries.reshape(8, SEG, HQ * HD)
    g = grad_out.reshape(8, SEG, HQ * HD)
    vmem = pl.BlockSpec(memory_space=pltpu.VMEM)
    hbm = pl.BlockSpec(memory_space=pl.ANY)
    unit = (ROWS, HD)
    results = pl.pallas_call(
        kernel,
        out_shape=(
            jax.ShapeDtypeStruct(q.shape, BF16),
            jax.ShapeDtypeStruct(q.shape, BF16),
            jax.ShapeDtypeStruct((1, 64, VT), BF16),
            jax.ShapeDtypeStruct((1, 64, VT), BF16),
        ),
        in_specs=[pl.BlockSpec(memory_space=pltpu.SMEM)] + [hbm] * 4,
        out_specs=(hbm, hbm, vmem, vmem),
        scratch_shapes=[pltpu.SMEM((64,), jnp.int32)]
        + [pltpu.VMEM((8, SEG, 2 * HALF * HD), BF16)] * 2
        + [pltpu.VMEM((KVH - 1, 8, SEG, 2 * HALF * HD), BF16)] * 2
        + [pltpu.VMEM((VT, KVH * HD), BF16)] * 2
        + [pltpu.VMEM((STEPS, 8, SEG, HALF * HD), BF16)] * 2
        + [pltpu.VMEM((STEPS, 3, 4) + unit, BF16)] * 4
        + [pltpu.VMEM((STEPS, 4, 4) + unit, BF16)] * 8
        + [pltpu.VMEM((KVH, JP, HD), BF16)] * 2
        + [pltpu.VMEM((KVH, HD, JP), BF16)] * 2
        + [pltpu.VMEM((16,) + unit, BF16)] * 2
        + [pltpu.VMEM((SLOTS,) + unit, BF16)] * 2
        + [
            pltpu.VMEM((JP, WIDE), F32),
            pltpu.VMEM((JP, WIDE), BF16),
            pltpu.VMEM((JP, HD), F32),
            pltpu.VMEM((JP, HD), F32),
            pltpu.VMEM((KVH - 1, 2, VT16, HD), BF16),
            pltpu.VMEM((KVH - 1, 2, VT16, HD), BF16),
            pltpu.VMEM((2, VT16, HD), BF16),
            pltpu.VMEM((2, VT16, HD), BF16),
        ]
        + [
            pltpu.SemaphoreType.DMA((4,)),
            pltpu.SemaphoreType.DMA((4, STEPS)),
            pltpu.SemaphoreType.DMA((4,)),
            pltpu.SemaphoreType.DMA((2, STEPS)),
        ]
        + [pltpu.SemaphoreType.DMA((KVH - 1,))] * 2
        + [pltpu.SemaphoreType.DMA] * 2
        + [
            pltpu.SemaphoreType.DMA((2,)),
            pltpu.SemaphoreType.DMA((2,)),
            pltpu.SemaphoreType.DMA((2,)),
            pltpu.SemaphoreType.DMA((2,)),
        ],
        compiler_params=pltpu.CompilerParams(
            collective_id=0, has_side_effects=True, vmem_limit_bytes=62 * 1024 * 1024
        ),
    )(reads.T, q, g, keys, values)
    attended, grad_queries, grad_keys, grad_values = pl.pallas_call(
        copy_out,
        out_shape=tuple(jax.ShapeDtypeStruct(r.shape, r.dtype) for r in results),
        in_specs=[hbm] * 4,
        out_specs=(hbm,) * 4,
        scratch_shapes=[pltpu.VMEM(r.shape, r.dtype) for r in results]
        + [pltpu.SemaphoreType.DMA((2, 4, 2))],
    )(*results)
    return (
        attended.reshape(queries.shape),
        grad_queries.reshape(queries.shape),
        jnp.swapaxes(grad_keys, 1, 2),
        jnp.swapaxes(grad_values, 1, 2),
    )


def solution(mesh):
    placed = (
        P(("seq", "enc"), None),
        P("enc", None, None),
        P("enc", None, None),
        P(),
        P(("seq", "enc"), None),
    )
    return jax.shard_map(
        per_device,
        mesh=mesh,
        in_specs=placed,
        out_specs=(
            P(("seq", "enc"), None),
            P(("seq", "enc"), None),
            P("enc", None, "seq"),
            P("enc", None, "seq"),
        ),
        check_vma=False,
    )
```

```python
import functools

import jax
import jax.numpy as jnp
from jax import lax
from jax.experimental import pallas as pl
from jax.experimental.pallas import tpu as pltpu
from jax.sharding import PartitionSpec as P

HQ = 32
KVH = 4
HD = 128
HALF = HQ // KVH // 2
SEG = 16
ROWS = HALF * SEG
STEPS = 2 * KVH
SLOTS = 12
WIDE = SLOTS * ROWS
VT = 1601
VT16 = 1616
JP = 1664
LOG2E = 1.4426950408889634
MESH = pl.DeviceIdType.MESH
BF16 = jnp.bfloat16
F32 = jnp.float32
CHUNKS = [(j, min(256, JP - j)) for j in range(0, JP, 256)]
NT = (((1,), (1,)), ((), ()))
IN, OUT = (0, 1), (2, 3)
AHEAD = 4
T_SEND, T_SRC, T_OK, T_POS = 0, 16, 32, 48


def kernel(
    reads_hbm, q_hbm, g_hbm, k_hbm, v_hbm, att_out, gq_out, gk_out, gv_out, end_o, end_d,
    reads, tab, q_0, g_0, q_in, g_in, k_in, v_in, att_v, gq_v, gk_v, gv_v,
    a_q, a_g, a_o, a_d, m_q, m_g, m_o, m_d, r_q, r_g, r_o, r_d,
    kh, vh, kt, vt, stage_q, stage_g, pack_o, pack_d, s_scr, p_scr, k_acc, v_acc,
    z_send, z_recv, c_send, c_recv,
    s1, w1, s2, w2, zs, zw, cs, cw, l0, ls, lo, lk, le, lr,
):
    sq = lax.axis_index("seq")
    en = lax.axis_index("enc")
    z, core = sq // 2, sq % 2
    x, y = en // 4, en % 4
    scale = HD ** (-0.5)

    first = (a_q, a_g, a_o, a_d)
    middle = (m_q, m_g, m_o, m_d)
    last = (r_q, r_g, r_o, r_d)
    own = [(x, y), (y, x), (x, y), (y, x)]

    def peer(axis, d):
        if axis == 0:
            return (sq, ((x + d) % 4) * 4 + y)
        return (sq, x * 4 + (y + d) % 4)

    def hop1(ten, s, d):
        return pltpu.make_async_remote_copy(
            src_ref=first[ten].at[s, d - 1],
            dst_ref=middle[ten].at[s, :, own[ten][0]],
            send_sem=s1.at[ten],
            recv_sem=w1.at[ten, s],
            device_id=peer(ten % 2, d),
            device_id_type=MESH,
        )

    def hop2(ten, s, d):
        b = own[ten][1]
        final = ten in OUT and isinstance(s, int) and s == STEPS - 1
        return pltpu.make_async_remote_copy(
            src_ref=middle[ten].at[s, (b + d) % 4],
            dst_ref=(end_o, end_d)[ten - 2].at[b] if final else last[ten].at[s, b],
            send_sem=s2.at[ten],
            recv_sem=w2.at[ten // 2, s],
            device_id=peer(1 - ten % 2, d),
            device_id_type=MESH,
        )

    def start1(pair, s):
        for d in (2, 1, 3):
            for ten in pair:
                hop1(ten, s, d).start()

    def await_recv(ref, sem):
        pltpu.make_async_remote_copy(
            src_ref=ref, dst_ref=ref, send_sem=s1.at[0], recv_sem=sem,
            device_id=peer(0, 1), device_id_type=MESH,
        ).wait_recv()

    def await_send(ref, sem):
        pltpu.make_async_remote_copy(
            src_ref=ref, dst_ref=ref, send_sem=sem, recv_sem=w1.at[0, 0],
            device_id=peer(0, 1), device_id_type=MESH,
        ).wait_send()

    def forward(pair, s):
        for ten in pair:
            await_recv(first[ten].at[s], w1.at[ten, s])
            for d in (2, 1, 3):
                hop2(ten, s, d).start()

    def arrive(pair, s):
        await_recv(first[pair[0]].at[pl.ds(0, 2)], w2.at[pair[0] // 2, s])

    def head_at(t):
        return (z + 1 + t) % 4

    def z_copy(t):
        return pltpu.make_async_remote_copy(
            src_ref=z_send.at[t],
            dst_ref=z_recv.at[t],
            send_sem=zs.at[t],
            recv_sem=zw.at[t],
            device_id=(head_at(t) * 2 + core, en),
            device_id_type=MESH,
        )

    def load(ten, t):
        cols = pl.ds(pl.multiple_of(head_at(t) * (2 * HALF * HD), 2 * HALF * HD), 2 * HALF * HD)
        src, dst = ((q_hbm, q_in), (g_hbm, g_in))[ten]
        if t == 0:
            return pltpu.make_async_copy(src.at[:, :, cols], (q_0, g_0)[ten], l0.at[ten])
        return pltpu.make_async_copy(src.at[:, :, cols], dst.at[t - 1], ls.at[ten])

    barrier = pltpu.get_barrier_semaphore()
    for d in (1, 2, 3):
        for target in (peer(0, d), peer(1, d), (((z + d) % 4) * 2 + core, en)):
            pl.semaphore_signal(barrier, inc=1, device_id=target, device_id_type=MESH)
    pl.semaphore_signal(barrier, inc=1, device_id=(z * 2 + 1 - core, en), device_id_type=MESH)
    table = pltpu.make_async_copy(reads_hbm, reads, lr)
    table.start()
    for t in range(KVH):
        load(0, t).start()
        load(1, t).start()
    loads_kv = [
        pltpu.make_async_copy(k_hbm.at[0], k_in, lk.at[0]),
        pltpu.make_async_copy(v_hbm.at[0], v_in, lk.at[1]),
    ]
    for copy in loads_kv:
        copy.start()

    block_row = sq * 16 + en
    table.wait()
    own_reads = [reads[r, block_row] for r in range(8)]
    for image in range(16):
        found = jnp.int32(0)
        for r in range(1, 8):
            found = jnp.where(own_reads[r] == image, r, found)
        tab[T_SEND + image] = found

    def pack_in(s, u, sources):
        cols = pl.ds(pl.multiple_of(u * (HALF * HD), HALF * HD), HALF * HD)
        for ten, src in ((0, sources[0]), (1, sources[1])):
            a_own = own[ten][0]
            for d in range(4):
                a = (a_own + d) % 4
                for b in range(4):
                    image = a * 4 + b if ten == 0 else b * 4 + a
                    block = src[tab[T_SEND + image], :, cols]
                    for g in range(HALF):
                        piece = block[:, g * HD : (g + 1) * HD]
                        rows = pl.ds(g * SEG, SEG)
                        if d == 0:
                            middle[ten][s, b, a_own, rows, :] = piece
                        else:
                            first[ten][s, d - 1, b, rows, :] = piece

    load(0, 0).wait()
    load(1, 0).wait()
    pack_in(0, 0, (q_0, g_0))
    pl.semaphore_wait(barrier, 10)
    start1(IN, 0)
    pack_in(1, 1, (q_0, g_0))
    start1(IN, 1)
    pltpu.make_async_copy(q_in, q_in, ls.at[0]).wait()
    pltpu.make_async_copy(g_in, g_in, ls.at[1]).wait()

    def send_in(s, carry):
        pack_in(s, s % 2, (q_in.at[s // 2 - 1], g_in.at[s // 2 - 1]))

        @pl.when(s < AHEAD)
        def _():
            start1(IN, s)

        return carry

    lax.fori_loop(2, STEPS, send_in, 0)

    count = jnp.int32(0)
    places = []
    for b in range(16):
        named = reads[0, sq * 16 + b] == en
        for r in range(1, 8):
            named = named | (reads[r, sq * 16 + b] == en)
        flag = jnp.where(named, 1, 0)
        tab[T_POS + b] = jnp.where(named, jnp.minimum(count, SLOTS - 1), 0)
        places.append(jnp.where(named, count, -1))
        count = count + flag
    for m in range(SLOTS):
        source = jnp.int32(0)
        for b in range(16):
            source = jnp.where(places[b] == m, b, source)
        tab[T_SRC + m] = source
        tab[T_OK + m] = jnp.where(count > m, 1, 0)

    forward(IN, 0)
    start1(IN, AHEAD)

    for copy in loads_kv:
        copy.wait()

    def heads(t, carry):
        cols = pl.ds(pl.multiple_of(head_at(t) * HD, HD), HD)
        for src, rows_ref, cols_ref in ((k_in, kh, kt), (v_in, vh, vt)):
            rows_ref[t, 0:1600, :] = src[0:1600, cols]
            tail = src[1600:VT, cols].astype(F32)
            mark = lax.broadcasted_iota(jnp.int32, (64, HD), 0) == 0
            rows_ref[t, 1600:JP, :] = jnp.where(
                mark, jnp.broadcast_to(tail, (64, HD)), 0.0
            ).astype(BF16)
            for j in range(0, JP, HD):
                cols_ref[t, :, j : j + HD] = rows_ref[t, j : j + HD, :].T
        return carry

    lax.fori_loop(0, 2, heads, 0)
    forward(IN, 1)
    start1(IN, AHEAD + 1)
    lax.fori_loop(2, KVH, heads, 0)
    forward(IN, 2)
    start1(IN, AHEAD + 2)

    def step(s, carry):
        t, u = s // 2, s % 2
        arrive(IN, s)
        for ten, stage in ((0, stage_q), (1, stage_g)):
            b_own = own[ten][1]
            for d in range(4):
                b = (b_own + d) % 4
                for a in range(4):
                    if d == 0:
                        stage[b * 4 + a] = middle[ten][s, b, a]
                    else:
                        stage[b * 4 + a] = last[ten][s, b, a]

        @pl.when(s + 3 < STEPS)
        def _():
            forward(IN, s + 3)

        @pl.when(s + 3 + AHEAD < STEPS)
        def _():
            start1(IN, s + 3 + AHEAD)

        @pl.when(u == 0)
        def _():
            k_acc[...] = jnp.zeros_like(k_acc)
            v_acc[...] = jnp.zeros_like(v_acc)

        q_parts, g_parts = [], []
        for m in range(SLOTS):
            source = tab[T_SRC + m]
            q_parts.append(stage_q[(source % 4) * 4 + source // 4])
            g_parts.append(jnp.where(tab[T_OK + m] > 0, stage_g[source].astype(F32), 0.0))
        q = jnp.concatenate(q_parts, axis=0)
        g_t = jnp.concatenate(g_parts, axis=0).T

        top = jnp.full((8, WIDE), -jnp.inf, F32)
        for j, n in CHUNKS:
            sc = lax.dot_general(kh[t, j : j + n, :], q, NT, preferred_element_type=F32)
            if j + n > VT:
                row = lax.broadcasted_iota(jnp.int32, sc.shape, 0) + j
                sc = jnp.where(row < VT, sc, -1e30)
            s_scr[j : j + n, :] = sc
            top = jnp.maximum(top, jnp.max(sc.reshape(n // 8, 8, WIDE), axis=0))
        c2 = scale * LOG2E
        top2 = jnp.max(top, axis=0, keepdims=True) * c2
        total = jnp.zeros((8, WIDE), F32)
        o_t = jnp.zeros((HD, WIDE), F32)
        for j, n in CHUNKS:
            p = jnp.exp2(s_scr[j : j + n, :] * c2 - top2)
            total += jnp.sum(p.reshape(n // 8, 8, WIDE), axis=0)
            p_b = p.astype(BF16)
            p_scr[j : j + n, :] = p_b
            o_t += jnp.dot(vt[t, :, j : j + n], p_b, preferred_element_type=F32)
        inv = 1.0 / jnp.sum(total, axis=0, keepdims=True)
        o_t = (o_t * inv).astype(BF16).astype(F32)
        pack_o[...] = o_t.T.astype(BF16).reshape(SLOTS, ROWS, HD)

        @pl.when(s > 1)
        def _():
            forward(OUT, s - 2)

        delta = jnp.sum(g_t * o_t, axis=0, keepdims=True) * inv
        g_s = (g_t * inv).astype(BF16)
        d_t = jnp.zeros((HD, WIDE), F32)
        for j, n in CHUNKS:
            dp = jnp.dot(vh[t, j : j + n, :], g_s, preferred_element_type=F32)
            p_b = p_scr[j : j + n, :]
            ds = (p_b.astype(F32) * (dp - delta)).astype(BF16)
            v_acc[j : j + n, :] += lax.dot_general(p_b, g_s, NT, preferred_element_type=F32)
            k_acc[j : j + n, :] += jnp.dot(ds, q, preferred_element_type=F32)
            d_t += jnp.dot(kt[t, :, j : j + n], ds, preferred_element_type=F32)
        pack_d[...] = (d_t * scale).T.astype(BF16).reshape(SLOTS, ROWS, HD)

        for ten, packed in ((2, pack_o), (3, pack_d)):
            a_own = own[ten][0]
            for d in range(4):
                a = (a_own + d) % 4
                for b in range(4):
                    block = a * 4 + b if ten == 2 else b * 4 + a
                    piece = packed[tab[T_POS + block]]
                    if d == 0:
                        middle[ten][s, b, a_own] = piece
                    else:
                        first[ten][s, d - 1, b] = piece
        start1(OUT, s)

        @pl.when((u == 1) & (t < KVH - 1))
        def _():
            z_send[t, 0] = (k_acc[0:VT16, :] * scale).astype(BF16)
            z_send[t, 1] = v_acc[0:VT16, :].astype(BF16)
            z_copy(t).start()

        return carry

    lax.fori_loop(0, STEPS, step, 0)

    parts = [(j, min(256, VT16 - j)) for j in range(0, VT16, 256)]
    for t in range(KVH - 1):
        z_copy(t).wait_recv()
    forward(OUT, STEPS - 2)
    for j, n in parts:
        rows = pl.ds(j, n)
        sums = [k_acc[rows, :] * scale, v_acc[rows, :]]
        for w, acc in ((0, k_acc), (1, v_acc)):
            for t in range(KVH - 1):
                sums[w] = sums[w] + z_recv[t, w, rows, :].astype(F32)
            acc[rows, :] = sums[w]
            c_send[w, rows, :] = sums[w].astype(BF16)
    core_copy = pltpu.make_async_remote_copy(
        src_ref=c_send,
        dst_ref=c_recv,
        send_sem=cs,
        recv_sem=cw,
        device_id=(z * 2 + 1 - core, en),
        device_id_type=MESH,
    )
    core_copy.start()
    forward(OUT, STEPS - 1)
    ends = []
    for ten, end in ((2, end_o), (3, end_d)):
        b_own = own[ten][1]
        ends.append(
            pltpu.make_async_copy(
                middle[ten].at[STEPS - 1, b_own], end.at[b_own], le.at[ten - 2]
            )
        )
    for copy in ends:
        copy.start()

    def out_copy(ten, s):
        cols = pl.ds(
            pl.multiple_of((head_at(s // 2) * 2 + s % 2) * (HALF * HD), HALF * HD), HALF * HD
        )
        src, dst = ((att_v, att_out), (gq_v, gq_out))[ten - 2]
        return pltpu.make_async_copy(src.at[s], dst.at[:, :, cols], lo.at[ten - 2])

    def collect(s, carry):
        arrive(OUT, s)
        for ten, stage, out in ((2, stage_q, att_v), (3, stage_g, gq_v)):
            b_own = own[ten][1]
            for d in range(4):
                b = (b_own + d) % 4
                for a in range(4):
                    src = middle[ten] if d == 0 else last[ten]
                    stage[b * 4 + a] = src[s, b, a]
            for r in range(8):
                image = reads[r, block_row]
                if ten == 2:
                    block = stage[(image % 4) * 4 + image // 4]
                else:
                    block = stage[image]
                for g in range(HALF):
                    out[s, r, :, g * HD : (g + 1) * HD] = block[g * SEG : (g + 1) * SEG, :]
            out_copy(ten, s).start()
        return carry

    lax.fori_loop(0, STEPS - 3, collect, 0)
    core_copy.wait_recv()
    for w, acc, out in ((0, k_acc, gk_v), (1, v_acc, gv_v)):
        for j in range(0, VT, HD):
            n = min(HD, VT16 - j)
            full = acc[j : j + n, :] + c_recv[w, j : j + n, :].astype(F32)
            if n < HD:
                full = jnp.concatenate([full, jnp.zeros((HD - n, HD), F32)], axis=0)
            turned = full.T
            half = jnp.where(core == 0, turned[0:64], turned[64:128]).astype(BF16)
            if j + HD > VT:
                out[0, :, j:VT] = half[:, 0 : VT - j]
            else:
                out[0, :, j : j + HD] = half
    gradients = [
        pltpu.make_async_copy(gk_v, gk_out, le.at[2]),
        pltpu.make_async_copy(gv_v, gv_out, le.at[3]),
    ]
    for copy in gradients:
        copy.start()
    for t in range(KVH - 1):
        z_copy(t).wait_send()
    core_copy.wait_send()
    lax.fori_loop(STEPS - 3, STEPS - 1, collect, 0)
    for ten in range(4):
        await_send(first[ten], s1.at[ten])
        if ten in IN:
            await_send(first[ten], s2.at[ten])
    pltpu.make_async_copy(att_v, att_v, lo.at[0]).wait()
    pltpu.make_async_copy(gq_v, gq_v, lo.at[1]).wait()
    for copy in ends + gradients:
        copy.wait()
    for ten in OUT:
        await_send(first[ten], s2.at[ten])
    arrive(OUT, STEPS - 1)


def copy_out(reads_hbm, att, gq, gk, gv, end_o, end_d, att_out, gq_out, gk_out, gv_out,
             reads, att_v, gq_v, gk_v, gv_v, end_ov, end_dv, into_sem, back_sem):
    sq = lax.axis_index("seq")
    en = lax.axis_index("enc")
    block_row = sq * 16 + en
    cols0 = ((sq // 2) * 2 + 1) * (HALF * HD)

    def into(src, dst, i):
        copy = pltpu.make_async_copy(src, dst, into_sem.at[i])
        copy.start()
        return copy

    ends = [into(reads_hbm, reads, 8), into(end_o, end_ov, 0), into(end_d, end_dv, 1)]
    halves = []
    for p in range(2):
        part = pl.ds(4 * p, 4)
        halves.append((p, 0, into(att.at[part], att_v.at[part], 2 + 2 * p)))
        halves.append((p, 1, into(gq.at[part], gq_v.at[part], 3 + 2 * p)))
    grads = [into(gk, gk_v, 6), into(gv, gv_v, 7)]
    for copy in ends:
        copy.wait()
    backs = []

    def back(src, dst, i):
        copy = pltpu.make_async_copy(src, dst, back_sem.at[i])
        copy.start()
        backs.append(copy)

    for p, w, copy in halves:
        copy.wait()
        part = pl.ds(4 * p, 4)
        buffer = (att_v, gq_v)[w]
        for r in range(4 * p, 4 * p + 4):
            image = reads[r, block_row]
            if w == 0:
                block = end_ov[image % 4, image // 4]
            else:
                block = end_dv[image // 4, image % 4]
            for g in range(HALF):
                cols = pl.ds(pl.multiple_of(cols0 + g * HD, HD), HD)
                buffer[r, :, cols] = block[g * SEG : (g + 1) * SEG, :]
        back(buffer.at[part], (att_out, gq_out)[w].at[part], 2 * p + w)
    for copy in grads:
        copy.wait()
    back(gk_v, gk_out, 4)
    back(gv_v, gv_out, 5)
    for copy in backs:
        copy.wait()


def per_device(queries, keys, values, reads, grad_out):
    q = queries.reshape(8, SEG, HQ * HD)
    g = grad_out.reshape(8, SEG, HQ * HD)
    hbm = pl.BlockSpec(memory_space=pl.ANY)
    unit = (ROWS, HD)
    results = pl.pallas_call(
        kernel,
        out_shape=(
            jax.ShapeDtypeStruct(q.shape, BF16),
            jax.ShapeDtypeStruct(q.shape, BF16),
            jax.ShapeDtypeStruct((1, 64, VT), BF16),
            jax.ShapeDtypeStruct((1, 64, VT), BF16),
            jax.ShapeDtypeStruct((4, 4) + unit, BF16),
            jax.ShapeDtypeStruct((4, 4) + unit, BF16),
        ),
        in_specs=[hbm] * 5,
        out_specs=(hbm,) * 6,
        scratch_shapes=[pltpu.SMEM((8, 128), jnp.int32), pltpu.SMEM((64,), jnp.int32)]
        + [pltpu.VMEM((8, SEG, 2 * HALF * HD), BF16)] * 2
        + [pltpu.VMEM((KVH - 1, 8, SEG, 2 * HALF * HD), BF16)] * 2
        + [pltpu.VMEM((VT, KVH * HD), BF16)] * 2
        + [pltpu.VMEM((STEPS - 1, 8, SEG, HALF * HD), BF16)] * 2
        + [pltpu.VMEM((1, 64, VT), BF16)] * 2
        + [pltpu.VMEM((STEPS, 3, 4) + unit, BF16)] * 4
        + [pltpu.VMEM((STEPS, 4, 4) + unit, BF16)] * 8
        + [pltpu.VMEM((KVH, JP, HD), BF16)] * 2
        + [pltpu.VMEM((KVH, HD, JP), BF16)] * 2
        + [pltpu.VMEM((16,) + unit, BF16)] * 2
        + [pltpu.VMEM((SLOTS,) + unit, BF16)] * 2
        + [
            pltpu.VMEM((JP, WIDE), F32),
            pltpu.VMEM((JP, WIDE), BF16),
            pltpu.VMEM((JP, HD), F32),
            pltpu.VMEM((JP, HD), F32),
            pltpu.VMEM((KVH - 1, 2, VT16, HD), BF16),
            pltpu.VMEM((KVH - 1, 2, VT16, HD), BF16),
            pltpu.VMEM((2, VT16, HD), BF16),
            pltpu.VMEM((2, VT16, HD), BF16),
        ]
        + [
            pltpu.SemaphoreType.DMA((4,)),
            pltpu.SemaphoreType.DMA((4, STEPS)),
            pltpu.SemaphoreType.DMA((4,)),
            pltpu.SemaphoreType.DMA((2, STEPS)),
        ]
        + [pltpu.SemaphoreType.DMA((KVH - 1,))] * 2
        + [pltpu.SemaphoreType.DMA] * 2
        + [
            pltpu.SemaphoreType.DMA((2,)),
            pltpu.SemaphoreType.DMA((2,)),
            pltpu.SemaphoreType.DMA((2,)),
            pltpu.SemaphoreType.DMA((2,)),
            pltpu.SemaphoreType.DMA((4,)),
            pltpu.SemaphoreType.DMA,
        ],
        compiler_params=pltpu.CompilerParams(
            collective_id=0, has_side_effects=True, vmem_limit_bytes=62 * 1024 * 1024
        ),
    )(reads.T, q, g, keys, values)
    attended, grad_queries, grad_keys, grad_values = pl.pallas_call(
        copy_out,
        out_shape=tuple(jax.ShapeDtypeStruct(r.shape, r.dtype) for r in results[:4]),
        in_specs=[hbm] * 7,
        out_specs=(hbm,) * 4,
        scratch_shapes=[pltpu.SMEM((8, 128), jnp.int32)]
        + [pltpu.VMEM(r.shape, r.dtype) for r in results]
        + [pltpu.SemaphoreType.DMA((9,)), pltpu.SemaphoreType.DMA((6,))],
    )(reads.T, *results)
    return (
        attended.reshape(queries.shape),
        grad_queries.reshape(queries.shape),
        jnp.swapaxes(grad_keys, 1, 2),
        jnp.swapaxes(grad_values, 1, 2),
    )


def solution(mesh):
    placed = (
        P(("seq", "enc"), None),
        P("enc", None, None),
        P("enc", None, None),
        P(),
        P(("seq", "enc"), None),
    )
    return jax.shard_map(
        per_device,
        mesh=mesh,
        in_specs=placed,
        out_specs=(
            P(("seq", "enc"), None),
            P(("seq", "enc"), None),
            P("enc", None, "seq"),
            P("enc", None, "seq"),
        ),
        check_vma=False,
    )
```

```python
import functools

import jax
import jax.numpy as jnp
from jax import lax
from jax.experimental import pallas as pl
from jax.experimental.pallas import tpu as pltpu
from jax.sharding import PartitionSpec as P

HQ = 32
KVH = 4
HD = 128
HALF = HQ // KVH // 2
SEG = 16
ROWS = HALF * SEG
STEPS = 2 * KVH
SLOTS = 12
WIDE = SLOTS * ROWS
VT = 1601
VT_MAIN = 1600
VT16 = 1616
JP = 1664
LOG2E = 1.4426950408889634
MESH = pl.DeviceIdType.MESH
BF16 = jnp.bfloat16
F32 = jnp.float32
CHUNKS = [(j, min(256, JP - j)) for j in range(0, JP, 256)]
NT = (((1,), (1,)), ((), ()))
IN, OUT = (0, 1), (2, 3)
AHEAD = 4
T_SEND, T_SRC, T_OK, T_POS = 0, 16, 32, 48


def kernel(
    reads_hbm, q_hbm, g_hbm, k_hbm, v_hbm, k_end, v_end, att_out, gq_out, gk_out, gv_out, end_o, end_d,
    reads, tab, q_0, g_0, q_in, g_in, k_in, v_in, att_v, gq_v, gk_v, gv_v,
    a_q, a_g, a_o, a_d, m_q, m_g, m_o, m_d, r_q, r_g, r_o, r_d,
    kh, vh, kt, vt, stage_q, stage_g, pack_o, pack_d, s_scr, p_scr, k_acc, v_acc,
    z_send, z_recv, c_send, c_recv,
    s1, w1, s2, w2, zs, zw, cs, cw, l0, ls, lo, lk, le, lr,
):
    sq = lax.axis_index("seq")
    en = lax.axis_index("enc")
    z, core = sq // 2, sq % 2
    x, y = en // 4, en % 4
    scale = HD ** (-0.5)

    first = (a_q, a_g, a_o, a_d)
    middle = (m_q, m_g, m_o, m_d)
    last = (r_q, r_g, r_o, r_d)
    own = [(x, y), (y, x), (x, y), (y, x)]

    def peer(axis, d):
        if axis == 0:
            return (sq, ((x + d) % 4) * 4 + y)
        return (sq, x * 4 + (y + d) % 4)

    def hop1(ten, s, d):
        return pltpu.make_async_remote_copy(
            src_ref=first[ten].at[s, d - 1],
            dst_ref=middle[ten].at[s, :, own[ten][0]],
            send_sem=s1.at[ten],
            recv_sem=w1.at[ten // 2, s],
            device_id=peer(ten % 2, d),
            device_id_type=MESH,
        )

    def hop2(ten, s, d):
        b = own[ten][1]
        final = ten in OUT and isinstance(s, int) and s == STEPS - 1
        return pltpu.make_async_remote_copy(
            src_ref=middle[ten].at[s, (b + d) % 4],
            dst_ref=(end_o, end_d)[ten - 2].at[b] if final else last[ten].at[s, b],
            send_sem=s2.at[ten],
            recv_sem=w2.at[ten // 2, s],
            device_id=peer(1 - ten % 2, d),
            device_id_type=MESH,
        )

    def start1(pair, s):
        for d in (2, 1, 3):
            for ten in pair:
                hop1(ten, s, d).start()

    def await_recv(ref, sem):
        pltpu.make_async_remote_copy(
            src_ref=ref, dst_ref=ref, send_sem=s1.at[0], recv_sem=sem,
            device_id=peer(0, 1), device_id_type=MESH,
        ).wait_recv()

    def await_send(ref, sem):
        pltpu.make_async_remote_copy(
            src_ref=ref, dst_ref=ref, send_sem=sem, recv_sem=w1.at[0, 0],
            device_id=peer(0, 1), device_id_type=MESH,
        ).wait_send()

    def forward(pair, s):
        await_recv(first[pair[0]].at[pl.ds(0, 2)], w1.at[pair[0] // 2, s])
        for d in (2, 1, 3):
            for ten in pair:
                hop2(ten, s, d).start()

    def arrive(pair, s):
        await_recv(first[pair[0]].at[pl.ds(0, 2)], w2.at[pair[0] // 2, s])

    def head_at(t):
        return (z + 1 + t) % 4

    def z_copy(t):
        return pltpu.make_async_remote_copy(
            src_ref=z_send.at[t],
            dst_ref=z_recv.at[t],
            send_sem=zs.at[t],
            recv_sem=zw.at[t],
            device_id=(head_at(t) * 2 + core, en),
            device_id_type=MESH,
        )

    def load(ten, t):
        cols = pl.ds(pl.multiple_of(head_at(t) * (2 * HALF * HD), 2 * HALF * HD), 2 * HALF * HD)
        src, dst = ((q_hbm, q_in), (g_hbm, g_in))[ten]
        if t == 0:
            return pltpu.make_async_copy(src.at[:, :, cols], (q_0, g_0)[ten], l0.at[ten])
        return pltpu.make_async_copy(src.at[:, :, cols], dst.at[t - 1], ls.at[ten])

    table = pltpu.make_async_copy(reads_hbm, reads, lr)
    table.start()
    load(0, 0).start()
    load(1, 0).start()
    barrier = pltpu.get_barrier_semaphore()
    for d in (1, 2, 3):
        for target in (peer(0, d), peer(1, d), (((z + d) % 4) * 2 + core, en)):
            pl.semaphore_signal(barrier, inc=1, device_id=target, device_id_type=MESH)
    pl.semaphore_signal(barrier, inc=1, device_id=(z * 2 + 1 - core, en), device_id_type=MESH)
    for t in range(1, KVH):
        load(0, t).start()
        load(1, t).start()
    loads_kv = [
        pltpu.make_async_copy(k_hbm.at[0, pl.ds(0, VT_MAIN)], k_in, lk.at[0]),
        pltpu.make_async_copy(v_hbm.at[0, pl.ds(0, VT_MAIN)], v_in, lk.at[1]),
    ]
    for copy in loads_kv:
        copy.start()

    block_row = sq * 16 + en
    table.wait()
    own_reads = [reads[r, block_row] for r in range(8)]
    for image in range(16):
        found = jnp.int32(0)
        for r in range(1, 8):
            found = jnp.where(own_reads[r] == image, r, found)
        tab[T_SEND + image] = found

    def pack_in(s, u, sources, tens=IN):
        cols = pl.ds(pl.multiple_of(u * (HALF * HD), HALF * HD), HALF * HD)
        for ten in tens:
            src = sources[ten]
            a_own = own[ten][0]
            for d in range(4):
                a = (a_own + d) % 4
                for b in range(4):
                    image = a * 4 + b if ten == 0 else b * 4 + a
                    block = src[tab[T_SEND + image], :, cols]
                    for g in range(HALF):
                        piece = block[:, g * HD : (g + 1) * HD]
                        rows = pl.ds(g * SEG, SEG)
                        if d == 0:
                            middle[ten][s, b, a_own, rows, :] = piece
                        else:
                            first[ten][s, d - 1, b, rows, :] = piece

    load(0, 0).wait()
    load(1, 0).wait()
    pack_in(0, 0, (q_0, g_0), (0,))
    pl.semaphore_wait(barrier, 10)
    start1((0,), 0)
    pack_in(0, 0, (q_0, g_0), (1,))
    start1((1,), 0)
    pack_in(1, 1, (q_0, g_0))
    start1(IN, 1)
    pltpu.make_async_copy(q_in, q_in, ls.at[0]).wait()
    pltpu.make_async_copy(g_in, g_in, ls.at[1]).wait()

    def send_in(s, carry):
        pack_in(s, s % 2, (q_in.at[s // 2 - 1], g_in.at[s // 2 - 1]))

        @pl.when(s < AHEAD)
        def _():
            start1(IN, s)

        return carry

    lax.fori_loop(2, STEPS, send_in, 0)

    count = jnp.int32(0)
    places = []
    for b in range(16):
        named = reads[0, sq * 16 + b] == en
        for r in range(1, 8):
            named = named | (reads[r, sq * 16 + b] == en)
        flag = jnp.where(named, 1, 0)
        tab[T_POS + b] = jnp.where(named, jnp.minimum(count, SLOTS - 1), 0)
        places.append(jnp.where(named, count, -1))
        count = count + flag
    for m in range(SLOTS):
        source = jnp.int32(0)
        for b in range(16):
            source = jnp.where(places[b] == m, b, source)
        tab[T_SRC + m] = source
        tab[T_OK + m] = jnp.where(count > m, 1, 0)

    forward(IN, 0)
    start1(IN, AHEAD)

    for copy in loads_kv:
        copy.wait()

    def heads(t, carry):
        cols = pl.ds(pl.multiple_of(head_at(t) * HD, HD), HD)
        for src, end, rows_ref, cols_ref in ((k_in, k_end, kh, kt), (v_in, v_end, vh, vt)):
            rows_ref[t, 0:VT_MAIN, :] = src[:, cols]
            tail = end[0, :, cols].astype(F32)
            mark = lax.broadcasted_iota(jnp.int32, tail.shape, 0) == 0
            rows_ref[t, VT_MAIN:VT16, :] = jnp.where(mark, tail, 0.0).astype(BF16)
            rows_ref[t, VT16:JP, :] = jnp.zeros((JP - VT16, HD), BF16)
            for j in range(0, JP, HD):
                cols_ref[t, :, j : j + HD] = rows_ref[t, j : j + HD, :].T
        return carry

    lax.fori_loop(0, 2, heads, 0)
    forward(IN, 1)
    start1(IN, AHEAD + 1)
    lax.fori_loop(2, KVH, heads, 0)
    forward(IN, 2)
    start1(IN, AHEAD + 2)

    def step(s, carry):
        t, u = s // 2, s % 2
        arrive(IN, s)
        for ten, stage in ((0, stage_q), (1, stage_g)):
            b_own = own[ten][1]
            for d in range(4):
                b = (b_own + d) % 4
                for a in range(4):
                    if d == 0:
                        stage[b * 4 + a] = middle[ten][s, b, a]
                    else:
                        stage[b * 4 + a] = last[ten][s, b, a]

        @pl.when(s + 3 < STEPS)
        def _():
            forward(IN, s + 3)

        @pl.when(s + 3 + AHEAD < STEPS)
        def _():
            start1(IN, s + 3 + AHEAD)

        @pl.when(u == 0)
        def _():
            k_acc[...] = jnp.zeros_like(k_acc)
            v_acc[...] = jnp.zeros_like(v_acc)

        q_parts, g_parts = [], []
        for m in range(SLOTS):
            source = tab[T_SRC + m]
            q_parts.append(stage_q[(source % 4) * 4 + source // 4])
            g_parts.append(jnp.where(tab[T_OK + m] > 0, stage_g[source].astype(F32), 0.0))
        q = jnp.concatenate(q_parts, axis=0)
        g_t = jnp.concatenate(g_parts, axis=0).T

        top = jnp.full((8, WIDE), -jnp.inf, F32)
        for j, n in CHUNKS:
            sc = lax.dot_general(kh[t, j : j + n, :], q, NT, preferred_element_type=F32)
            if j + n > VT:
                row = lax.broadcasted_iota(jnp.int32, sc.shape, 0) + j
                sc = jnp.where(row < VT, sc, -1e30)
            s_scr[j : j + n, :] = sc
            top = jnp.maximum(top, jnp.max(sc.reshape(n // 8, 8, WIDE), axis=0))
        c2 = scale * LOG2E
        top2 = jnp.max(top, axis=0, keepdims=True) * c2
        total = jnp.zeros((8, WIDE), F32)
        o_t = jnp.zeros((HD, WIDE), F32)
        for j, n in CHUNKS:
            p = jnp.exp2(s_scr[j : j + n, :] * c2 - top2)
            total += jnp.sum(p.reshape(n // 8, 8, WIDE), axis=0)
            p_b = p.astype(BF16)
            p_scr[j : j + n, :] = p_b
            o_t += jnp.dot(vt[t, :, j : j + n], p_b, preferred_element_type=F32)
        inv = 1.0 / jnp.sum(total, axis=0, keepdims=True)
        o_t = (o_t * inv).astype(BF16).astype(F32)
        pack_o[...] = o_t.T.astype(BF16).reshape(SLOTS, ROWS, HD)

        @pl.when(s > 1)
        def _():
            forward(OUT, s - 2)

        g_s = (g_t * inv).astype(BF16)
        delta = jnp.sum(g_s.astype(F32) * o_t, axis=0, keepdims=True)
        d_t = jnp.zeros((HD, WIDE), F32)
        for j, n in CHUNKS:
            dp = jnp.dot(vh[t, j : j + n, :], g_s, preferred_element_type=F32)
            p_b = p_scr[j : j + n, :]
            ds = (p_b.astype(F32) * (dp - delta)).astype(BF16)
            v_acc[j : j + n, :] += lax.dot_general(p_b, g_s, NT, preferred_element_type=F32)
            k_acc[j : j + n, :] += jnp.dot(ds, q, preferred_element_type=F32)
            d_t += jnp.dot(kt[t, :, j : j + n], ds, preferred_element_type=F32)
        pack_d[...] = (d_t * scale).T.astype(BF16).reshape(SLOTS, ROWS, HD)

        for ten, packed in ((2, pack_o), (3, pack_d)):
            a_own = own[ten][0]
            for d in range(4):
                a = (a_own + d) % 4
                for b in range(4):
                    block = a * 4 + b if ten == 2 else b * 4 + a
                    piece = packed[tab[T_POS + block]]
                    if d == 0:
                        middle[ten][s, b, a_own] = piece
                    else:
                        first[ten][s, d - 1, b] = piece
        start1(OUT, s)

        @pl.when((u == 1) & (t < KVH - 1))
        def _():
            z_send[t, 0] = (k_acc[0:VT16, :] * scale).astype(BF16)
            z_send[t, 1] = v_acc[0:VT16, :].astype(BF16)
            z_copy(t).start()

        return carry

    lax.fori_loop(0, STEPS, step, 0)

    parts = [(j, min(256, VT16 - j)) for j in range(0, VT16, 256)]
    for t in range(KVH - 1):
        z_copy(t).wait_recv()
    forward(OUT, STEPS - 2)
    for j, n in parts:
        rows = pl.ds(j, n)
        sums = [k_acc[rows, :] * scale, v_acc[rows, :]]
        for w, acc in ((0, k_acc), (1, v_acc)):
            for t in range(KVH - 1):
                sums[w] = sums[w] + z_recv[t, w, rows, :].astype(F32)
            acc[rows, :] = sums[w]
            c_send[w, rows, :] = sums[w].astype(BF16)
    core_copy = pltpu.make_async_remote_copy(
        src_ref=c_send,
        dst_ref=c_recv,
        send_sem=cs,
        recv_sem=cw,
        device_id=(z * 2 + 1 - core, en),
        device_id_type=MESH,
    )
    core_copy.start()
    forward(OUT, STEPS - 1)
    ends = []
    for ten, end in ((2, end_o), (3, end_d)):
        b_own = own[ten][1]
        ends.append(
            pltpu.make_async_copy(
                middle[ten].at[STEPS - 1, b_own], end.at[b_own], le.at[ten - 2]
            )
        )
    for copy in ends:
        copy.start()

    def out_copy(ten, s):
        cols = pl.ds(
            pl.multiple_of((head_at(s // 2) * 2 + s % 2) * (HALF * HD), HALF * HD), HALF * HD
        )
        src, dst = ((att_v, att_out), (gq_v, gq_out))[ten - 2]
        return pltpu.make_async_copy(src.at[s], dst.at[:, :, cols], lo.at[ten - 2])

    def collect(s, carry):
        arrive(OUT, s)
        for ten, stage, out in ((2, stage_q, att_v), (3, stage_g, gq_v)):
            b_own = own[ten][1]
            for d in range(4):
                b = (b_own + d) % 4
                for a in range(4):
                    src = middle[ten] if d == 0 else last[ten]
                    stage[b * 4 + a] = src[s, b, a]
            for r in range(8):
                image = reads[r, block_row]
                if ten == 2:
                    block = stage[(image % 4) * 4 + image // 4]
                else:
                    block = stage[image]
                for g in range(HALF):
                    out[s, r, :, g * HD : (g + 1) * HD] = block[g * SEG : (g + 1) * SEG, :]
            out_copy(ten, s).start()
        return carry

    lax.fori_loop(0, STEPS - 3, collect, 0)
    core_copy.wait_recv()
    for w, acc, out in ((0, k_acc, gk_v), (1, v_acc, gv_v)):
        for j in range(0, VT, HD):
            n = min(HD, VT16 - j)
            full = acc[j : j + n, :] + c_recv[w, j : j + n, :].astype(F32)
            if n < HD:
                full = jnp.concatenate([full, jnp.zeros((HD - n, HD), F32)], axis=0)
            turned = full.T
            half = jnp.where(core == 0, turned[0:64], turned[64:128]).astype(BF16)
            if j + HD > VT:
                out[0, :, j:VT] = half[:, 0 : VT - j]
            else:
                out[0, :, j : j + HD] = half
    gradients = [
        pltpu.make_async_copy(gk_v, gk_out, le.at[2]),
        pltpu.make_async_copy(gv_v, gv_out, le.at[3]),
    ]
    for copy in gradients:
        copy.start()
    for t in range(KVH - 1):
        z_copy(t).wait_send()
    core_copy.wait_send()
    lax.fori_loop(STEPS - 3, STEPS - 1, collect, 0)
    for ten in range(4):
        await_send(first[ten], s1.at[ten])
        if ten in IN:
            await_send(first[ten], s2.at[ten])
    pltpu.make_async_copy(att_v, att_v, lo.at[0]).wait()
    pltpu.make_async_copy(gq_v, gq_v, lo.at[1]).wait()
    for copy in ends + gradients:
        copy.wait()
    for ten in OUT:
        await_send(first[ten], s2.at[ten])
    arrive(OUT, STEPS - 1)


def copy_out(reads_hbm, att, gq, gk, gv, end_o, end_d, att_out, gq_out, gk_out, gv_out,
             reads, att_v, gq_v, gk_v, gv_v, end_ov, end_dv, into_sem, back_sem):
    sq = lax.axis_index("seq")
    en = lax.axis_index("enc")
    block_row = sq * 16 + en
    cols0 = ((sq // 2) * 2 + 1) * (HALF * HD)

    def into(src, dst, i):
        copy = pltpu.make_async_copy(src, dst, into_sem.at[i])
        copy.start()
        return copy

    ends = [into(reads_hbm, reads, 8), into(end_o, end_ov, 0), into(end_d, end_dv, 1)]
    halves = []
    for p in range(2):
        part = pl.ds(4 * p, 4)
        halves.append((p, 0, into(att.at[part], att_v.at[part], 2 + 2 * p)))
        halves.append((p, 1, into(gq.at[part], gq_v.at[part], 3 + 2 * p)))
    grads = [into(gk, gk_v, 6), into(gv, gv_v, 7)]
    for copy in ends:
        copy.wait()
    backs = []

    def back(src, dst, i):
        copy = pltpu.make_async_copy(src, dst, back_sem.at[i])
        copy.start()
        backs.append(copy)

    for p, w, copy in halves:
        copy.wait()
        part = pl.ds(4 * p, 4)
        buffer = (att_v, gq_v)[w]
        for r in range(4 * p, 4 * p + 4):
            image = reads[r, block_row]
            if w == 0:
                block = end_ov[image % 4, image // 4]
            else:
                block = end_dv[image // 4, image % 4]
            for g in range(HALF):
                cols = pl.ds(pl.multiple_of(cols0 + g * HD, HD), HD)
                buffer[r, :, cols] = block[g * SEG : (g + 1) * SEG, :]
        back(buffer.at[part], (att_out, gq_out)[w].at[part], 2 * p + w)
    for copy in grads:
        copy.wait()
    back(gk_v, gk_out, 4)
    back(gv_v, gv_out, 5)
    for copy in backs:
        copy.wait()


def per_device(queries, keys, values, reads, grad_out):
    q = queries.reshape(8, SEG, HQ * HD)
    g = grad_out.reshape(8, SEG, HQ * HD)
    hbm = pl.BlockSpec(memory_space=pl.ANY)
    unit = (ROWS, HD)
    results = pl.pallas_call(
        kernel,
        grid=(1,),
        out_shape=(
            jax.ShapeDtypeStruct(q.shape, BF16),
            jax.ShapeDtypeStruct(q.shape, BF16),
            jax.ShapeDtypeStruct((1, 64, VT), BF16),
            jax.ShapeDtypeStruct((1, 64, VT), BF16),
            jax.ShapeDtypeStruct((4, 4) + unit, BF16),
            jax.ShapeDtypeStruct((4, 4) + unit, BF16),
        ),
        in_specs=[hbm] * 5 + [pl.BlockSpec((1, 16, KVH * HD), lambda i: (0, VT_MAIN // 16, 0))] * 2,
        out_specs=(hbm,) * 6,
        scratch_shapes=[pltpu.SMEM((8, 128), jnp.int32), pltpu.SMEM((64,), jnp.int32)]
        + [pltpu.VMEM((8, SEG, 2 * HALF * HD), BF16)] * 2
        + [pltpu.VMEM((KVH - 1, 8, SEG, 2 * HALF * HD), BF16)] * 2
        + [pltpu.VMEM((VT_MAIN, KVH * HD), BF16)] * 2
        + [pltpu.VMEM((STEPS - 1, 8, SEG, HALF * HD), BF16)] * 2
        + [pltpu.VMEM((1, 64, VT), BF16)] * 2
        + [pltpu.VMEM((STEPS, 3, 4) + unit, BF16)] * 4
        + [pltpu.VMEM((STEPS, 4, 4) + unit, BF16)] * 8
        + [pltpu.VMEM((KVH, JP, HD), BF16)] * 2
        + [pltpu.VMEM((KVH, HD, JP), BF16)] * 2
        + [pltpu.VMEM((16,) + unit, BF16)] * 2
        + [pltpu.VMEM((SLOTS,) + unit, BF16)] * 2
        + [
            pltpu.VMEM((JP, WIDE), F32),
            pltpu.VMEM((JP, WIDE), BF16),
            pltpu.VMEM((JP, HD), F32),
            pltpu.VMEM((JP, HD), F32),
            pltpu.VMEM((KVH - 1, 2, VT16, HD), BF16),
            pltpu.VMEM((KVH - 1, 2, VT16, HD), BF16),
            pltpu.VMEM((2, VT16, HD), BF16),
            pltpu.VMEM((2, VT16, HD), BF16),
        ]
        + [
            pltpu.SemaphoreType.DMA((4,)),
            pltpu.SemaphoreType.DMA((2, STEPS)),
            pltpu.SemaphoreType.DMA((4,)),
            pltpu.SemaphoreType.DMA((2, STEPS)),
        ]
        + [pltpu.SemaphoreType.DMA((KVH - 1,))] * 2
        + [pltpu.SemaphoreType.DMA] * 2
        + [
            pltpu.SemaphoreType.DMA((2,)),
            pltpu.SemaphoreType.DMA((2,)),
            pltpu.SemaphoreType.DMA((2,)),
            pltpu.SemaphoreType.DMA((2,)),
            pltpu.SemaphoreType.DMA((4,)),
            pltpu.SemaphoreType.DMA,
        ],
        compiler_params=pltpu.CompilerParams(
            collective_id=0, has_side_effects=True, vmem_limit_bytes=62 * 1024 * 1024
        ),
    )(reads.T, q, g, keys, values, keys, values)
    attended, grad_queries, grad_keys, grad_values = pl.pallas_call(
        copy_out,
        out_shape=tuple(jax.ShapeDtypeStruct(r.shape, r.dtype) for r in results[:4]),
        in_specs=[hbm] * 7,
        out_specs=(hbm,) * 4,
        scratch_shapes=[pltpu.SMEM((8, 128), jnp.int32)]
        + [pltpu.VMEM(r.shape, r.dtype) for r in results]
        + [pltpu.SemaphoreType.DMA((9,)), pltpu.SemaphoreType.DMA((6,))],
    )(reads.T, *results)
    return (
        attended.reshape(queries.shape),
        grad_queries.reshape(queries.shape),
        jnp.swapaxes(grad_keys, 1, 2),
        jnp.swapaxes(grad_values, 1, 2),
    )


def solution(mesh):
    placed = (
        P(("seq", "enc"), None),
        P("enc", None, None),
        P("enc", None, None),
        P(),
        P(("seq", "enc"), None),
    )
    return jax.shard_map(
        per_device,
        mesh=mesh,
        in_specs=placed,
        out_specs=(
            P(("seq", "enc"), None),
            P(("seq", "enc"), None),
            P("enc", None, "seq"),
            P("enc", None, "seq"),
        ),
        check_vma=False,
    )
```

```python
import functools

import jax
import jax.numpy as jnp
from jax import lax
from jax.experimental import pallas as pl
from jax.experimental.pallas import tpu as pltpu
from jax.sharding import PartitionSpec as P

HQ = 32
KVH = 4
HD = 128
HALF = HQ // KVH // 2
SEG = 16
ROWS = HALF * SEG
STEPS = 2 * KVH
SLOTS = 12
WIDE = SLOTS * ROWS
VT = 1601
VT_MAIN = 1600
VT16 = 1616
JP = 1664
LOG2E = 1.4426950408889634
MESH = pl.DeviceIdType.MESH
BF16 = jnp.bfloat16
F32 = jnp.float32
CHUNKS = [(j, min(256, JP - j)) for j in range(0, JP, 256)]
NT = (((1,), (1,)), ((), ()))
IN, OUT = (0, 1), (2, 3)
AHEAD = 4
T_SEND, T_SRC, T_OK, T_POS = 0, 16, 32, 48


def kernel(
    reads_hbm, q_hbm, g_hbm, k_in, v_in, att_out, gq_out, gk_out, gv_out, end_o, end_d,
    reads, tab, q_0, g_0, q_in, g_in, att_v, gq_v, gk_v, gv_v,
    a_q, a_g, a_o, a_d, m_q, m_g, m_o, m_d, r_q, r_g, r_o, r_d,
    kh, vh, kt, vt, stage_q, stage_g, pack_o, pack_d, s_scr, p_scr, k_acc, v_acc,
    z_send, z_recv, c_send, c_recv,
    s1, w1, s2, w2, zs, zw, cs, cw, l0, ls, lo, le, lr,
):
    sq = lax.axis_index("seq")
    en = lax.axis_index("enc")
    z, core = sq // 2, sq % 2
    x, y = en // 4, en % 4
    scale = HD ** (-0.5)

    first = (a_q, a_g, a_o, a_d)
    middle = (m_q, m_g, m_o, m_d)
    last = (r_q, r_g, r_o, r_d)
    own = [(x, y), (y, x), (x, y), (y, x)]

    def peer(axis, d):
        if axis == 0:
            return (sq, ((x + d) % 4) * 4 + y)
        return (sq, x * 4 + (y + d) % 4)

    def hop1(ten, s, d):
        return pltpu.make_async_remote_copy(
            src_ref=first[ten].at[s, d - 1],
            dst_ref=middle[ten].at[s, :, own[ten][0]],
            send_sem=s1.at[ten],
            recv_sem=w1.at[ten // 2, s],
            device_id=peer(ten % 2, d),
            device_id_type=MESH,
        )

    def hop2(ten, s, d):
        b = own[ten][1]
        final = ten in OUT and isinstance(s, int) and s == STEPS - 1
        return pltpu.make_async_remote_copy(
            src_ref=middle[ten].at[s, (b + d) % 4],
            dst_ref=(end_o, end_d)[ten - 2].at[b] if final else last[ten].at[s, b],
            send_sem=s2.at[ten],
            recv_sem=w2.at[ten // 2, s],
            device_id=peer(1 - ten % 2, d),
            device_id_type=MESH,
        )

    def start1(pair, s):
        for d in (2, 1, 3):
            for ten in pair:
                hop1(ten, s, d).start()

    def await_recv(ref, sem):
        pltpu.make_async_remote_copy(
            src_ref=ref, dst_ref=ref, send_sem=s1.at[0], recv_sem=sem,
            device_id=peer(0, 1), device_id_type=MESH,
        ).wait_recv()

    def await_send(ref, sem):
        pltpu.make_async_remote_copy(
            src_ref=ref, dst_ref=ref, send_sem=sem, recv_sem=w1.at[0, 0],
            device_id=peer(0, 1), device_id_type=MESH,
        ).wait_send()

    def forward(pair, s):
        await_recv(first[pair[0]].at[pl.ds(0, 2)], w1.at[pair[0] // 2, s])
        for d in (2, 1, 3):
            for ten in pair:
                hop2(ten, s, d).start()

    def arrive(pair, s):
        await_recv(first[pair[0]].at[pl.ds(0, 2)], w2.at[pair[0] // 2, s])

    def head_at(t):
        return (z + 1 + t) % 4

    def z_copy(t):
        return pltpu.make_async_remote_copy(
            src_ref=z_send.at[t],
            dst_ref=z_recv.at[t],
            send_sem=zs.at[t],
            recv_sem=zw.at[t],
            device_id=(head_at(t) * 2 + core, en),
            device_id_type=MESH,
        )

    def load(ten, t):
        cols = pl.ds(pl.multiple_of(head_at(t) * (2 * HALF * HD), 2 * HALF * HD), 2 * HALF * HD)
        src, dst = ((q_hbm, q_in), (g_hbm, g_in))[ten]
        if t == 0:
            return pltpu.make_async_copy(src.at[:, :, cols], (q_0, g_0)[ten], l0.at[ten])
        return pltpu.make_async_copy(src.at[:, :, cols], dst.at[t - 1], ls.at[ten])

    table = pltpu.make_async_copy(reads_hbm, reads, lr)
    table.start()
    load(0, 0).start()
    load(1, 0).start()
    barrier = pltpu.get_barrier_semaphore()
    for d in (1, 2, 3):
        for target in (peer(0, d), peer(1, d), (((z + d) % 4) * 2 + core, en)):
            pl.semaphore_signal(barrier, inc=1, device_id=target, device_id_type=MESH)
    pl.semaphore_signal(barrier, inc=1, device_id=(z * 2 + 1 - core, en), device_id_type=MESH)
    for t in range(1, KVH):
        load(0, t).start()
        load(1, t).start()
    block_row = sq * 16 + en
    table.wait()
    own_reads = [reads[r, block_row] for r in range(8)]
    for image in range(16):
        found = jnp.int32(0)
        for r in range(1, 8):
            found = jnp.where(own_reads[r] == image, r, found)
        tab[T_SEND + image] = found

    def pack_in(s, u, sources, tens=IN):
        cols = pl.ds(pl.multiple_of(u * (HALF * HD), HALF * HD), HALF * HD)
        for ten in tens:
            src = sources[ten]
            a_own = own[ten][0]
            for d in range(4):
                a = (a_own + d) % 4
                for b in range(4):
                    image = a * 4 + b if ten == 0 else b * 4 + a
                    block = src[tab[T_SEND + image], :, cols]
                    for g in range(HALF):
                        piece = block[:, g * HD : (g + 1) * HD]
                        rows = pl.ds(g * SEG, SEG)
                        if d == 0:
                            middle[ten][s, b, a_own, rows, :] = piece
                        else:
                            first[ten][s, d - 1, b, rows, :] = piece

    load(0, 0).wait()
    load(1, 0).wait()
    pack_in(0, 0, (q_0, g_0), (0,))
    pl.semaphore_wait(barrier, 10)
    start1((0,), 0)
    pack_in(0, 0, (q_0, g_0), (1,))
    start1((1,), 0)
    pack_in(1, 1, (q_0, g_0))
    start1(IN, 1)
    pltpu.make_async_copy(q_in, q_in, ls.at[0]).wait()
    pltpu.make_async_copy(g_in, g_in, ls.at[1]).wait()

    def send_in(s, carry):
        pack_in(s, s % 2, (q_in.at[s // 2 - 1], g_in.at[s // 2 - 1]))

        @pl.when(s < AHEAD)
        def _():
            start1(IN, s)

        return carry

    lax.fori_loop(2, STEPS, send_in, 0)

    count = jnp.int32(0)
    places = []
    for b in range(16):
        named = reads[0, sq * 16 + b] == en
        for r in range(1, 8):
            named = named | (reads[r, sq * 16 + b] == en)
        flag = jnp.where(named, 1, 0)
        tab[T_POS + b] = jnp.where(named, jnp.minimum(count, SLOTS - 1), 0)
        places.append(jnp.where(named, count, -1))
        count = count + flag
    for m in range(SLOTS):
        source = jnp.int32(0)
        for b in range(16):
            source = jnp.where(places[b] == m, b, source)
        tab[T_SRC + m] = source
        tab[T_OK + m] = jnp.where(count > m, 1, 0)

    forward(IN, 0)
    start1(IN, AHEAD)

    def heads(t, carry):
        cols = pl.ds(pl.multiple_of(head_at(t) * HD, HD), HD)
        for src, rows_ref, cols_ref in ((k_in, kh, kt), (v_in, vh, vt)):
            rows_ref[t, 0:VT_MAIN, :] = src[0, 0:VT_MAIN, cols]
            tail = src[0, VT_MAIN:VT, cols].astype(F32)
            mark = lax.broadcasted_iota(jnp.int32, (64, HD), 0) == 0
            rows_ref[t, VT_MAIN:JP, :] = jnp.where(
                mark, jnp.broadcast_to(tail, (64, HD)), 0.0
            ).astype(BF16)
            for j in range(0, JP, HD):
                cols_ref[t, :, j : j + HD] = rows_ref[t, j : j + HD, :].T
        return carry

    lax.fori_loop(0, 2, heads, 0)
    forward(IN, 1)
    start1(IN, AHEAD + 1)
    lax.fori_loop(2, KVH, heads, 0)
    forward(IN, 2)
    start1(IN, AHEAD + 2)

    def step(s, carry):
        t, u = s // 2, s % 2
        arrive(IN, s)
        for ten, stage in ((0, stage_q), (1, stage_g)):
            b_own = own[ten][1]
            for d in range(4):
                b = (b_own + d) % 4
                for a in range(4):
                    if d == 0:
                        stage[b * 4 + a] = middle[ten][s, b, a]
                    else:
                        stage[b * 4 + a] = last[ten][s, b, a]

        @pl.when(s + 3 < STEPS)
        def _():
            forward(IN, s + 3)

        @pl.when(s + 3 + AHEAD < STEPS)
        def _():
            start1(IN, s + 3 + AHEAD)

        @pl.when(u == 0)
        def _():
            k_acc[...] = jnp.zeros_like(k_acc)
            v_acc[...] = jnp.zeros_like(v_acc)

        q_parts, g_parts = [], []
        for m in range(SLOTS):
            source = tab[T_SRC + m]
            q_parts.append(stage_q[(source % 4) * 4 + source // 4])
            g_parts.append(jnp.where(tab[T_OK + m] > 0, stage_g[source].astype(F32), 0.0))
        q = jnp.concatenate(q_parts, axis=0)
        g_t = jnp.concatenate(g_parts, axis=0).T

        top = jnp.full((8, WIDE), -jnp.inf, F32)
        for j, n in CHUNKS:
            sc = lax.dot_general(kh[t, j : j + n, :], q, NT, preferred_element_type=F32)
            if j + n > VT:
                row = lax.broadcasted_iota(jnp.int32, sc.shape, 0) + j
                sc = jnp.where(row < VT, sc, -1e30)
            s_scr[j : j + n, :] = sc
            top = jnp.maximum(top, jnp.max(sc.reshape(n // 8, 8, WIDE), axis=0))
        c2 = scale * LOG2E
        top2 = jnp.max(top, axis=0, keepdims=True) * c2
        total = jnp.zeros((8, WIDE), F32)
        o_t = jnp.zeros((HD, WIDE), F32)
        for j, n in CHUNKS:
            p = jnp.exp2(s_scr[j : j + n, :] * c2 - top2)
            total += jnp.sum(p.reshape(n // 8, 8, WIDE), axis=0)
            p_b = p.astype(BF16)
            p_scr[j : j + n, :] = p_b
            o_t += jnp.dot(vt[t, :, j : j + n], p_b, preferred_element_type=F32)
        inv = 1.0 / jnp.sum(total, axis=0, keepdims=True)
        o_t = (o_t * inv).astype(BF16).astype(F32)
        pack_o[...] = o_t.T.astype(BF16).reshape(SLOTS, ROWS, HD)

        @pl.when(s > 1)
        def _():
            forward(OUT, s - 2)

        g_s = (g_t * inv).astype(BF16)
        delta = jnp.sum(g_s.astype(F32) * o_t, axis=0, keepdims=True)
        d_t = jnp.zeros((HD, WIDE), F32)
        for j, n in CHUNKS:
            dp = jnp.dot(vh[t, j : j + n, :], g_s, preferred_element_type=F32)
            p_b = p_scr[j : j + n, :]
            ds = (p_b.astype(F32) * (dp - delta)).astype(BF16)
            v_acc[j : j + n, :] += lax.dot_general(p_b, g_s, NT, preferred_element_type=F32)
            k_acc[j : j + n, :] += jnp.dot(ds, q, preferred_element_type=F32)
            d_t += jnp.dot(kt[t, :, j : j + n], ds, preferred_element_type=F32)
        pack_d[...] = (d_t * scale).T.astype(BF16).reshape(SLOTS, ROWS, HD)

        for ten, packed in ((2, pack_o), (3, pack_d)):
            a_own = own[ten][0]
            for d in range(4):
                a = (a_own + d) % 4
                for b in range(4):
                    block = a * 4 + b if ten == 2 else b * 4 + a
                    piece = packed[tab[T_POS + block]]
                    if d == 0:
                        middle[ten][s, b, a_own] = piece
                    else:
                        first[ten][s, d - 1, b] = piece
        start1(OUT, s)

        @pl.when((u == 1) & (t < KVH - 1))
        def _():
            z_send[t, 0] = (k_acc[0:VT16, :] * scale).astype(BF16)
            z_send[t, 1] = v_acc[0:VT16, :].astype(BF16)
            z_copy(t).start()

        return carry

    lax.fori_loop(0, STEPS, step, 0)

    parts = [(j, min(256, VT16 - j)) for j in range(0, VT16, 256)]
    for t in range(KVH - 1):
        z_copy(t).wait_recv()
    forward(OUT, STEPS - 2)
    for j, n in parts:
        rows = pl.ds(j, n)
        sums = [k_acc[rows, :] * scale, v_acc[rows, :]]
        for w, acc in ((0, k_acc), (1, v_acc)):
            for t in range(KVH - 1):
                sums[w] = sums[w] + z_recv[t, w, rows, :].astype(F32)
            acc[rows, :] = sums[w]
            c_send[w, rows, :] = sums[w].astype(BF16)
    core_copy = pltpu.make_async_remote_copy(
        src_ref=c_send,
        dst_ref=c_recv,
        send_sem=cs,
        recv_sem=cw,
        device_id=(z * 2 + 1 - core, en),
        device_id_type=MESH,
    )
    core_copy.start()
    forward(OUT, STEPS - 1)
    ends = []
    for ten, end in ((2, end_o), (3, end_d)):
        b_own = own[ten][1]
        ends.append(
            pltpu.make_async_copy(
                middle[ten].at[STEPS - 1, b_own], end.at[b_own], le.at[ten - 2]
            )
        )
    for copy in ends:
        copy.start()

    def out_copy(ten, s):
        cols = pl.ds(
            pl.multiple_of((head_at(s // 2) * 2 + s % 2) * (HALF * HD), HALF * HD), HALF * HD
        )
        src, dst = ((att_v, att_out), (gq_v, gq_out))[ten - 2]
        return pltpu.make_async_copy(src.at[s], dst.at[:, :, cols], lo.at[ten - 2])

    def collect(s, carry):
        arrive(OUT, s)
        for ten, stage, out in ((2, stage_q, att_v), (3, stage_g, gq_v)):
            b_own = own[ten][1]
            for d in range(4):
                b = (b_own + d) % 4
                for a in range(4):
                    src = middle[ten] if d == 0 else last[ten]
                    stage[b * 4 + a] = src[s, b, a]
            for r in range(8):
                image = reads[r, block_row]
                if ten == 2:
                    block = stage[(image % 4) * 4 + image // 4]
                else:
                    block = stage[image]
                for g in range(HALF):
                    out[s, r, :, g * HD : (g + 1) * HD] = block[g * SEG : (g + 1) * SEG, :]
            out_copy(ten, s).start()
        return carry

    lax.fori_loop(0, STEPS - 3, collect, 0)
    core_copy.wait_recv()
    for w, acc, out in ((0, k_acc, gk_v), (1, v_acc, gv_v)):
        for j in range(0, VT, HD):
            n = min(HD, VT16 - j)
            full = acc[j : j + n, :] + c_recv[w, j : j + n, :].astype(F32)
            if n < HD:
                full = jnp.concatenate([full, jnp.zeros((HD - n, HD), F32)], axis=0)
            turned = full.T
            half = jnp.where(core == 0, turned[0:64], turned[64:128]).astype(BF16)
            if j + HD > VT:
                out[0, :, j:VT] = half[:, 0 : VT - j]
            else:
                out[0, :, j : j + HD] = half
    gradients = [
        pltpu.make_async_copy(gk_v, gk_out, le.at[2]),
        pltpu.make_async_copy(gv_v, gv_out, le.at[3]),
    ]
    for copy in gradients:
        copy.start()
    for t in range(KVH - 1):
        z_copy(t).wait_send()
    core_copy.wait_send()
    lax.fori_loop(STEPS - 3, STEPS - 1, collect, 0)
    for ten in range(4):
        await_send(first[ten], s1.at[ten])
        if ten in IN:
            await_send(first[ten], s2.at[ten])
    pltpu.make_async_copy(att_v, att_v, lo.at[0]).wait()
    pltpu.make_async_copy(gq_v, gq_v, lo.at[1]).wait()
    for copy in ends + gradients:
        copy.wait()
    for ten in OUT:
        await_send(first[ten], s2.at[ten])
    arrive(OUT, STEPS - 1)


def copy_out(reads_hbm, att, gq, gk, gv, end_o, end_d, att_out, gq_out, gk_out, gv_out,
             reads, att_v, gq_v, gk_v, gv_v, end_ov, end_dv, into_sem, back_sem):
    sq = lax.axis_index("seq")
    en = lax.axis_index("enc")
    block_row = sq * 16 + en
    cols0 = ((sq // 2) * 2 + 1) * (HALF * HD)

    def into(src, dst, i):
        copy = pltpu.make_async_copy(src, dst, into_sem.at[i])
        copy.start()
        return copy

    ends = [into(reads_hbm, reads, 8), into(end_o, end_ov, 0), into(end_d, end_dv, 1)]
    halves = []
    for p in range(2):
        part = pl.ds(4 * p, 4)
        halves.append((p, 0, into(att.at[part], att_v.at[part], 2 + 2 * p)))
        halves.append((p, 1, into(gq.at[part], gq_v.at[part], 3 + 2 * p)))
    grads = [into(gk, gk_v, 6), into(gv, gv_v, 7)]
    for copy in ends:
        copy.wait()
    backs = []

    def back(src, dst, i):
        copy = pltpu.make_async_copy(src, dst, back_sem.at[i])
        copy.start()
        backs.append(copy)

    for p, w, copy in halves:
        copy.wait()
        part = pl.ds(4 * p, 4)
        buffer = (att_v, gq_v)[w]
        for r in range(4 * p, 4 * p + 4):
            image = reads[r, block_row]
            if w == 0:
                block = end_ov[image % 4, image // 4]
            else:
                block = end_dv[image // 4, image % 4]
            for g in range(HALF):
                cols = pl.ds(pl.multiple_of(cols0 + g * HD, HD), HD)
                buffer[r, :, cols] = block[g * SEG : (g + 1) * SEG, :]
        back(buffer.at[part], (att_out, gq_out)[w].at[part], 2 * p + w)
    for copy in grads:
        copy.wait()
    back(gk_v, gk_out, 4)
    back(gv_v, gv_out, 5)
    for copy in backs:
        copy.wait()


def per_device(queries, keys, values, reads, grad_out):
    q = queries.reshape(8, SEG, HQ * HD)
    g = grad_out.reshape(8, SEG, HQ * HD)
    hbm = pl.BlockSpec(memory_space=pl.ANY)
    unit = (ROWS, HD)
    results = pl.pallas_call(
        kernel,
        out_shape=(
            jax.ShapeDtypeStruct(q.shape, BF16),
            jax.ShapeDtypeStruct(q.shape, BF16),
            jax.ShapeDtypeStruct((1, 64, VT), BF16),
            jax.ShapeDtypeStruct((1, 64, VT), BF16),
            jax.ShapeDtypeStruct((4, 4) + unit, BF16),
            jax.ShapeDtypeStruct((4, 4) + unit, BF16),
        ),
        in_specs=[hbm] * 3 + [pl.BlockSpec(memory_space=pltpu.VMEM)] * 2,
        out_specs=(hbm,) * 6,
        scratch_shapes=[pltpu.SMEM((8, 128), jnp.int32), pltpu.SMEM((64,), jnp.int32)]
        + [pltpu.VMEM((8, SEG, 2 * HALF * HD), BF16)] * 2
        + [pltpu.VMEM((KVH - 1, 8, SEG, 2 * HALF * HD), BF16)] * 2
        + [pltpu.VMEM((STEPS - 1, 8, SEG, HALF * HD), BF16)] * 2
        + [pltpu.VMEM((1, 64, VT), BF16)] * 2
        + [pltpu.VMEM((STEPS, 3, 4) + unit, BF16)] * 4
        + [pltpu.VMEM((STEPS, 4, 4) + unit, BF16)] * 8
        + [pltpu.VMEM((KVH, JP, HD), BF16)] * 2
        + [pltpu.VMEM((KVH, HD, JP), BF16)] * 2
        + [pltpu.VMEM((16,) + unit, BF16)] * 2
        + [pltpu.VMEM((SLOTS,) + unit, BF16)] * 2
        + [
            pltpu.VMEM((JP, WIDE), F32),
            pltpu.VMEM((JP, WIDE), BF16),
            pltpu.VMEM((JP, HD), F32),
            pltpu.VMEM((JP, HD), F32),
            pltpu.VMEM((KVH - 1, 2, VT16, HD), BF16),
            pltpu.VMEM((KVH - 1, 2, VT16, HD), BF16),
            pltpu.VMEM((2, VT16, HD), BF16),
            pltpu.VMEM((2, VT16, HD), BF16),
        ]
        + [
            pltpu.SemaphoreType.DMA((4,)),
            pltpu.SemaphoreType.DMA((2, STEPS)),
            pltpu.SemaphoreType.DMA((4,)),
            pltpu.SemaphoreType.DMA((2, STEPS)),
        ]
        + [pltpu.SemaphoreType.DMA((KVH - 1,))] * 2
        + [pltpu.SemaphoreType.DMA] * 2
        + [
            pltpu.SemaphoreType.DMA((2,)),
            pltpu.SemaphoreType.DMA((2,)),
            pltpu.SemaphoreType.DMA((2,)),
            pltpu.SemaphoreType.DMA((4,)),
            pltpu.SemaphoreType.DMA,
        ],
        compiler_params=pltpu.CompilerParams(
            collective_id=0, has_side_effects=True, vmem_limit_bytes=62 * 1024 * 1024
        ),
    )(reads.T, q, g, keys, values)
    attended, grad_queries, grad_keys, grad_values = pl.pallas_call(
        copy_out,
        out_shape=tuple(jax.ShapeDtypeStruct(r.shape, r.dtype) for r in results[:4]),
        in_specs=[hbm] * 7,
        out_specs=(hbm,) * 4,
        scratch_shapes=[pltpu.SMEM((8, 128), jnp.int32)]
        + [pltpu.VMEM(r.shape, r.dtype) for r in results]
        + [pltpu.SemaphoreType.DMA((9,)), pltpu.SemaphoreType.DMA((6,))],
    )(reads.T, *results)
    return (
        attended.reshape(queries.shape),
        grad_queries.reshape(queries.shape),
        jnp.swapaxes(grad_keys, 1, 2),
        jnp.swapaxes(grad_values, 1, 2),
    )


def solution(mesh):
    placed = (
        P(("seq", "enc"), None),
        P("enc", None, None),
        P("enc", None, None),
        P(),
        P(("seq", "enc"), None),
    )
    return jax.shard_map(
        per_device,
        mesh=mesh,
        in_specs=placed,
        out_specs=(
            P(("seq", "enc"), None),
            P(("seq", "enc"), None),
            P("enc", None, "seq"),
            P("enc", None, "seq"),
        ),
        check_vma=False,
    )
```

```python
import functools

import jax
import jax.numpy as jnp
from jax import lax
from jax.experimental import pallas as pl
from jax.experimental.pallas import tpu as pltpu
from jax.sharding import PartitionSpec as P

HQ = 32
KVH = 4
HD = 128
HALF = HQ // KVH // 2
SEG = 16
ROWS = HALF * SEG
STEPS = 2 * KVH
SLOTS = 12
WIDE = SLOTS * ROWS
VT = 1601
VT_MAIN = 1600
VT16 = 1616
JP = 1664
LOG2E = 1.4426950408889634
MESH = pl.DeviceIdType.MESH
BF16 = jnp.bfloat16
F32 = jnp.float32
CHUNKS = [(j, min(256, JP - j)) for j in range(0, JP, 256)]
NT = (((1,), (1,)), ((), ()))
IN, OUT = (0, 1), (2, 3)
AHEAD = 4
T_SEND, T_SRC, T_OK, T_POS = 0, 16, 32, 48


def kernel(
    reads_hbm, q_hbm, g_hbm, k_hbm, v_hbm, k_end, v_end, att_out, gq_out, gk_out, gv_out, end_o, end_d,
    reads, tab, q_0, g_0, q_in, g_in, k_in, v_in, att_v, gq_v, gk_v, gv_v,
    a_q, a_g, a_o, a_d, m_q, m_g, m_o, m_d, r_q, r_g, r_o, r_d,
    kh, vh, kt, vt, stage_q, stage_g, pack_o, pack_d, s_scr, p_scr, k_acc, v_acc,
    z_send, z_recv, c_send, c_recv,
    s1, w1, s2, w2, zs, zw, cs, cw, l0, ls, lo, lk, le, lr,
):
    sq = lax.axis_index("seq")
    en = lax.axis_index("enc")
    z, core = sq // 2, sq % 2
    x, y = en // 4, en % 4
    scale = HD ** (-0.5)

    first = (a_q, a_g, a_o, a_d)
    middle = (m_q, m_g, m_o, m_d)
    last = (r_q, r_g, r_o, r_d)
    own = [(x, y), (y, x), (x, y), (y, x)]

    def peer(axis, d):
        if axis == 0:
            return (sq, ((x + d) % 4) * 4 + y)
        return (sq, x * 4 + (y + d) % 4)

    def hop1(ten, s, d):
        return pltpu.make_async_remote_copy(
            src_ref=first[ten].at[s, d - 1],
            dst_ref=middle[ten].at[s, :, own[ten][0]],
            send_sem=s1.at[ten],
            recv_sem=w1.at[ten // 2, s],
            device_id=peer(ten % 2, d),
            device_id_type=MESH,
        )

    def hop2(ten, s, d):
        b = own[ten][1]
        final = ten in OUT and isinstance(s, int) and s == STEPS - 1
        return pltpu.make_async_remote_copy(
            src_ref=middle[ten].at[s, (b + d) % 4],
            dst_ref=(end_o, end_d)[ten - 2].at[b] if final else last[ten].at[s, b],
            send_sem=s2.at[ten],
            recv_sem=w2.at[ten // 2, s],
            device_id=peer(1 - ten % 2, d),
            device_id_type=MESH,
        )

    def start1(pair, s):
        for d in (2, 1, 3):
            for ten in pair:
                hop1(ten, s, d).start()

    def await_recv(ref, sem):
        pltpu.make_async_remote_copy(
            src_ref=ref, dst_ref=ref, send_sem=s1.at[0], recv_sem=sem,
            device_id=peer(0, 1), device_id_type=MESH,
        ).wait_recv()

    def await_send(ref, sem):
        pltpu.make_async_remote_copy(
            src_ref=ref, dst_ref=ref, send_sem=sem, recv_sem=w1.at[0, 0],
            device_id=peer(0, 1), device_id_type=MESH,
        ).wait_send()

    def forward(pair, s):
        await_recv(first[pair[0]].at[pl.ds(0, 2)], w1.at[pair[0] // 2, s])
        for d in (2, 1, 3):
            for ten in pair:
                hop2(ten, s, d).start()

    def arrive(pair, s):
        await_recv(first[pair[0]].at[pl.ds(0, 2)], w2.at[pair[0] // 2, s])

    def head_at(t):
        return (z + 1 + t) % 4

    def z_copy(t):
        return pltpu.make_async_remote_copy(
            src_ref=z_send.at[t],
            dst_ref=z_recv.at[t],
            send_sem=zs.at[t],
            recv_sem=zw.at[t],
            device_id=(head_at(t) * 2 + core, en),
            device_id_type=MESH,
        )

    def load(ten, t):
        cols = pl.ds(pl.multiple_of(head_at(t) * (2 * HALF * HD), 2 * HALF * HD), 2 * HALF * HD)
        src, dst = ((q_hbm, q_in), (g_hbm, g_in))[ten]
        if t == 0:
            return pltpu.make_async_copy(src.at[:, :, cols], (q_0, g_0)[ten], l0.at[ten])
        return pltpu.make_async_copy(src.at[:, :, cols], dst.at[t - 1], ls.at[ten])

    barrier = pltpu.get_barrier_semaphore()
    for d in (2, 1, 3):
        pl.semaphore_signal(
            barrier, inc=1, device_id=(((z + d) % 4) * 2 + core, en), device_id_type=MESH
        )
    for d in (2, 1, 3):
        for target in (peer(0, d), peer(1, d)):
            pl.semaphore_signal(barrier, inc=1, device_id=target, device_id_type=MESH)
    pl.semaphore_signal(barrier, inc=1, device_id=(z * 2 + 1 - core, en), device_id_type=MESH)
    table = pltpu.make_async_copy(reads_hbm, reads, lr)
    table.start()
    load(0, 0).start()
    load(1, 0).start()
    for t in range(1, KVH):
        load(0, t).start()
        load(1, t).start()
    loads_kv = [
        pltpu.make_async_copy(k_hbm.at[0, pl.ds(0, VT_MAIN)], k_in, lk.at[0]),
        pltpu.make_async_copy(v_hbm.at[0, pl.ds(0, VT_MAIN)], v_in, lk.at[1]),
    ]
    for copy in loads_kv:
        copy.start()

    block_row = sq * 16 + en
    table.wait()
    own_reads = [reads[r, block_row] for r in range(8)]
    for image in range(16):
        found = jnp.int32(0)
        for r in range(1, 8):
            found = jnp.where(own_reads[r] == image, r, found)
        tab[T_SEND + image] = found

    def pack_in(s, u, sources, tens=IN):
        cols = pl.ds(pl.multiple_of(u * (HALF * HD), HALF * HD), HALF * HD)
        for ten in tens:
            src = sources[ten]
            a_own = own[ten][0]
            for d in range(4):
                a = (a_own + d) % 4
                for b in range(4):
                    image = a * 4 + b if ten == 0 else b * 4 + a
                    block = src[tab[T_SEND + image], :, cols]
                    for g in range(HALF):
                        piece = block[:, g * HD : (g + 1) * HD]
                        rows = pl.ds(g * SEG, SEG)
                        if d == 0:
                            middle[ten][s, b, a_own, rows, :] = piece
                        else:
                            first[ten][s, d - 1, b, rows, :] = piece

    load(0, 0).wait()
    load(1, 0).wait()
    pack_in(0, 0, (q_0, g_0), (0,))
    pl.semaphore_wait(barrier, 10)
    start1((0,), 0)
    pack_in(0, 0, (q_0, g_0), (1,))
    start1((1,), 0)
    pack_in(1, 1, (q_0, g_0))
    start1(IN, 1)
    pltpu.make_async_copy(q_in, q_in, ls.at[0]).wait()
    pltpu.make_async_copy(g_in, g_in, ls.at[1]).wait()

    def send_in(s, carry):
        pack_in(s, s % 2, (q_in.at[s // 2 - 1], g_in.at[s // 2 - 1]))

        @pl.when(s < AHEAD)
        def _():
            start1(IN, s)

        return carry

    lax.fori_loop(2, STEPS, send_in, 0)

    count = jnp.int32(0)
    places = []
    for b in range(16):
        named = reads[0, sq * 16 + b] == en
        for r in range(1, 8):
            named = named | (reads[r, sq * 16 + b] == en)
        flag = jnp.where(named, 1, 0)
        tab[T_POS + b] = jnp.where(named, jnp.minimum(count, SLOTS - 1), 0)
        places.append(jnp.where(named, count, -1))
        count = count + flag
    for m in range(SLOTS):
        source = jnp.int32(0)
        for b in range(16):
            source = jnp.where(places[b] == m, b, source)
        tab[T_SRC + m] = source
        tab[T_OK + m] = jnp.where(count > m, 1, 0)

    forward(IN, 0)
    start1(IN, AHEAD)

    for copy in loads_kv:
        copy.wait()

    def heads(t, carry):
        cols = pl.ds(pl.multiple_of(head_at(t) * HD, HD), HD)
        for src, end, rows_ref, cols_ref in ((k_in, k_end, kh, kt), (v_in, v_end, vh, vt)):
            rows_ref[t, 0:VT_MAIN, :] = src[:, cols]
            tail = end[0, :, cols].astype(F32)
            mark = lax.broadcasted_iota(jnp.int32, tail.shape, 0) == 0
            rows_ref[t, VT_MAIN:VT16, :] = jnp.where(mark, tail, 0.0).astype(BF16)
            rows_ref[t, VT16:JP, :] = jnp.zeros((JP - VT16, HD), BF16)
            for j in range(0, JP, HD):
                cols_ref[t, :, j : j + HD] = rows_ref[t, j : j + HD, :].T
        return carry

    lax.fori_loop(0, 2, heads, 0)
    forward(IN, 1)
    start1(IN, AHEAD + 1)
    lax.fori_loop(2, KVH, heads, 0)
    forward(IN, 2)
    start1(IN, AHEAD + 2)

    def step(s, carry):
        t, u = s // 2, s % 2
        arrive(IN, s)
        for ten, stage in ((0, stage_q), (1, stage_g)):
            b_own = own[ten][1]
            for d in range(4):
                b = (b_own + d) % 4
                for a in range(4):
                    if d == 0:
                        stage[b * 4 + a] = middle[ten][s, b, a]
                    else:
                        stage[b * 4 + a] = last[ten][s, b, a]

        @pl.when(s + 3 < STEPS)
        def _():
            forward(IN, s + 3)

        @pl.when(s + 3 + AHEAD < STEPS)
        def _():
            start1(IN, s + 3 + AHEAD)

        @pl.when(u == 0)
        def _():
            k_acc[...] = jnp.zeros_like(k_acc)
            v_acc[...] = jnp.zeros_like(v_acc)

        q_parts, g_parts = [], []
        for m in range(SLOTS):
            source = tab[T_SRC + m]
            q_parts.append(stage_q[(source % 4) * 4 + source // 4])
            g_parts.append(jnp.where(tab[T_OK + m] > 0, stage_g[source].astype(F32), 0.0))
        q = jnp.concatenate(q_parts, axis=0)
        g_t = jnp.concatenate(g_parts, axis=0).T

        top = jnp.full((8, WIDE), -jnp.inf, F32)
        for j, n in CHUNKS:
            sc = lax.dot_general(kh[t, j : j + n, :], q, NT, preferred_element_type=F32)
            if j + n > VT:
                row = lax.broadcasted_iota(jnp.int32, sc.shape, 0) + j
                sc = jnp.where(row < VT, sc, -1e30)
            s_scr[j : j + n, :] = sc
            top = jnp.maximum(top, jnp.max(sc.reshape(n // 8, 8, WIDE), axis=0))
        c2 = scale * LOG2E
        top2 = jnp.max(top, axis=0, keepdims=True) * c2
        total = jnp.zeros((8, WIDE), F32)
        o_t = jnp.zeros((HD, WIDE), F32)
        for j, n in CHUNKS:
            p = jnp.exp2(s_scr[j : j + n, :] * c2 - top2)
            total += jnp.sum(p.reshape(n // 8, 8, WIDE), axis=0)
            p_b = p.astype(BF16)
            p_scr[j : j + n, :] = p_b
            o_t += jnp.dot(vt[t, :, j : j + n], p_b, preferred_element_type=F32)
        inv = 1.0 / jnp.sum(total, axis=0, keepdims=True)
        o_t = (o_t * inv).astype(BF16).astype(F32)
        pack_o[...] = o_t.T.astype(BF16).reshape(SLOTS, ROWS, HD)

        @pl.when(s > 1)
        def _():
            forward(OUT, s - 2)

        g_s = (g_t * inv).astype(BF16)
        delta = jnp.sum(g_s.astype(F32) * o_t, axis=0, keepdims=True)
        d_t = jnp.zeros((HD, WIDE), F32)
        for j, n in CHUNKS:
            dp = jnp.dot(vh[t, j : j + n, :], g_s, preferred_element_type=F32)
            p_b = p_scr[j : j + n, :]
            ds = (p_b.astype(F32) * (dp - delta)).astype(BF16)
            v_acc[j : j + n, :] += lax.dot_general(p_b, g_s, NT, preferred_element_type=F32)
            k_acc[j : j + n, :] += jnp.dot(ds, q, preferred_element_type=F32)
            d_t += jnp.dot(kt[t, :, j : j + n], ds, preferred_element_type=F32)
        pack_d[...] = (d_t * scale).T.astype(BF16).reshape(SLOTS, ROWS, HD)

        for ten, packed in ((2, pack_o), (3, pack_d)):
            a_own = own[ten][0]
            for d in range(4):
                a = (a_own + d) % 4
                for b in range(4):
                    block = a * 4 + b if ten == 2 else b * 4 + a
                    piece = packed[tab[T_POS + block]]
                    if d == 0:
                        middle[ten][s, b, a_own] = piece
                    else:
                        first[ten][s, d - 1, b] = piece
        start1(OUT, s)

        @pl.when((u == 1) & (t < KVH - 1))
        def _():
            z_send[t, 0] = (k_acc[0:VT16, :] * scale).astype(BF16)
            z_send[t, 1] = v_acc[0:VT16, :].astype(BF16)
            z_copy(t).start()

        return carry

    lax.fori_loop(0, STEPS, step, 0)

    parts = [(j, min(256, VT16 - j)) for j in range(0, VT16, 256)]
    for t in range(KVH - 1):
        z_copy(t).wait_recv()
    forward(OUT, STEPS - 2)
    for j, n in parts:
        rows = pl.ds(j, n)
        sums = [k_acc[rows, :] * scale, v_acc[rows, :]]
        for w, acc in ((0, k_acc), (1, v_acc)):
            for t in range(KVH - 1):
                sums[w] = sums[w] + z_recv[t, w, rows, :].astype(F32)
            acc[rows, :] = sums[w]
            c_send[w, rows, :] = sums[w].astype(BF16)
    core_copy = pltpu.make_async_remote_copy(
        src_ref=c_send,
        dst_ref=c_recv,
        send_sem=cs,
        recv_sem=cw,
        device_id=(z * 2 + 1 - core, en),
        device_id_type=MESH,
    )
    core_copy.start()
    forward(OUT, STEPS - 1)
    ends = []
    for ten, end in ((2, end_o), (3, end_d)):
        b_own = own[ten][1]
        ends.append(
            pltpu.make_async_copy(
                middle[ten].at[STEPS - 1, b_own], end.at[b_own], le.at[ten - 2]
            )
        )
    for copy in ends:
        copy.start()

    def out_copy(ten, s):
        cols = pl.ds(
            pl.multiple_of((head_at(s // 2) * 2 + s % 2) * (HALF * HD), HALF * HD), HALF * HD
        )
        src, dst = ((att_v, att_out), (gq_v, gq_out))[ten - 2]
        return pltpu.make_async_copy(src.at[s], dst.at[:, :, cols], lo.at[ten - 2])

    def collect(s, carry):
        arrive(OUT, s)
        for ten, stage, out in ((2, stage_q, att_v), (3, stage_g, gq_v)):
            b_own = own[ten][1]
            for d in range(4):
                b = (b_own + d) % 4
                for a in range(4):
                    src = middle[ten] if d == 0 else last[ten]
                    stage[b * 4 + a] = src[s, b, a]
            for r in range(8):
                image = reads[r, block_row]
                if ten == 2:
                    block = stage[(image % 4) * 4 + image // 4]
                else:
                    block = stage[image]
                for g in range(HALF):
                    out[s, r, :, g * HD : (g + 1) * HD] = block[g * SEG : (g + 1) * SEG, :]
            out_copy(ten, s).start()
        return carry

    lax.fori_loop(0, STEPS - 3, collect, 0)
    core_copy.wait_recv()
    for w, acc, out in ((0, k_acc, gk_v), (1, v_acc, gv_v)):
        for j in range(0, VT, HD):
            n = min(HD, VT16 - j)
            full = acc[j : j + n, :] + c_recv[w, j : j + n, :].astype(F32)
            if n < HD:
                full = jnp.concatenate([full, jnp.zeros((HD - n, HD), F32)], axis=0)
            turned = full.T
            half = jnp.where(core == 0, turned[0:64], turned[64:128]).astype(BF16)
            if j + HD > VT:
                out[0, :, j:VT] = half[:, 0 : VT - j]
            else:
                out[0, :, j : j + HD] = half
    gradients = [
        pltpu.make_async_copy(gk_v, gk_out, le.at[2]),
        pltpu.make_async_copy(gv_v, gv_out, le.at[3]),
    ]
    for copy in gradients:
        copy.start()
    for t in range(KVH - 1):
        z_copy(t).wait_send()
    core_copy.wait_send()
    lax.fori_loop(STEPS - 3, STEPS - 1, collect, 0)
    for ten in range(4):
        await_send(first[ten], s1.at[ten])
        if ten in IN:
            await_send(first[ten], s2.at[ten])
    pltpu.make_async_copy(att_v, att_v, lo.at[0]).wait()
    pltpu.make_async_copy(gq_v, gq_v, lo.at[1]).wait()
    for copy in ends + gradients:
        copy.wait()
    for ten in OUT:
        await_send(first[ten], s2.at[ten])
    arrive(OUT, STEPS - 1)


def copy_out(reads_hbm, att, gq, gk, gv, end_o, end_d, att_out, gq_out, gk_out, gv_out,
             reads, att_v, gq_v, gk_v, gv_v, end_ov, end_dv, into_sem, back_sem):
    sq = lax.axis_index("seq")
    en = lax.axis_index("enc")
    block_row = sq * 16 + en
    cols0 = ((sq // 2) * 2 + 1) * (HALF * HD)

    def into(src, dst, i):
        copy = pltpu.make_async_copy(src, dst, into_sem.at[i])
        copy.start()
        return copy

    ends = [into(reads_hbm, reads, 8), into(end_o, end_ov, 0), into(end_d, end_dv, 1)]
    halves = []
    for p in range(2):
        part = pl.ds(4 * p, 4)
        halves.append((p, 0, into(att.at[part], att_v.at[part], 2 + 2 * p)))
        halves.append((p, 1, into(gq.at[part], gq_v.at[part], 3 + 2 * p)))
    grads = [into(gk, gk_v, 6), into(gv, gv_v, 7)]
    for copy in ends:
        copy.wait()
    backs = []

    def back(src, dst, i):
        copy = pltpu.make_async_copy(src, dst, back_sem.at[i])
        copy.start()
        backs.append(copy)

    for p, w, copy in halves:
        copy.wait()
        part = pl.ds(4 * p, 4)
        buffer = (att_v, gq_v)[w]
        for r in range(4 * p, 4 * p + 4):
            image = reads[r, block_row]
            if w == 0:
                block = end_ov[image % 4, image // 4]
            else:
                block = end_dv[image // 4, image % 4]
            for g in range(HALF):
                cols = pl.ds(pl.multiple_of(cols0 + g * HD, HD), HD)
                buffer[r, :, cols] = block[g * SEG : (g + 1) * SEG, :]
        back(buffer.at[part], (att_out, gq_out)[w].at[part], 2 * p + w)
    for copy in grads:
        copy.wait()
    back(gk_v, gk_out, 4)
    back(gv_v, gv_out, 5)
    for copy in backs:
        copy.wait()


def per_device(queries, keys, values, reads, grad_out):
    q = queries.reshape(8, SEG, HQ * HD)
    g = grad_out.reshape(8, SEG, HQ * HD)
    hbm = pl.BlockSpec(memory_space=pl.ANY)
    unit = (ROWS, HD)
    results = pl.pallas_call(
        kernel,
        grid=(1,),
        out_shape=(
            jax.ShapeDtypeStruct(q.shape, BF16),
            jax.ShapeDtypeStruct(q.shape, BF16),
            jax.ShapeDtypeStruct((1, 64, VT), BF16),
            jax.ShapeDtypeStruct((1, 64, VT), BF16),
            jax.ShapeDtypeStruct((4, 4) + unit, BF16),
            jax.ShapeDtypeStruct((4, 4) + unit, BF16),
        ),
        in_specs=[hbm] * 5 + [pl.BlockSpec((1, 16, KVH * HD), lambda i: (0, VT_MAIN // 16, 0))] * 2,
        out_specs=(hbm,) * 6,
        scratch_shapes=[pltpu.SMEM((8, 128), jnp.int32), pltpu.SMEM((64,), jnp.int32)]
        + [pltpu.VMEM((8, SEG, 2 * HALF * HD), BF16)] * 2
        + [pltpu.VMEM((KVH - 1, 8, SEG, 2 * HALF * HD), BF16)] * 2
        + [pltpu.VMEM((VT_MAIN, KVH * HD), BF16)] * 2
        + [pltpu.VMEM((STEPS - 1, 8, SEG, HALF * HD), BF16)] * 2
        + [pltpu.VMEM((1, 64, VT), BF16)] * 2
        + [pltpu.VMEM((STEPS, 3, 4) + unit, BF16)] * 4
        + [pltpu.VMEM((STEPS, 4, 4) + unit, BF16)] * 8
        + [pltpu.VMEM((KVH, JP, HD), BF16)] * 2
        + [pltpu.VMEM((KVH, HD, JP), BF16)] * 2
        + [pltpu.VMEM((16,) + unit, BF16)] * 2
        + [pltpu.VMEM((SLOTS,) + unit, BF16)] * 2
        + [
            pltpu.VMEM((JP, WIDE), F32),
            pltpu.VMEM((JP, WIDE), BF16),
            pltpu.VMEM((JP, HD), F32),
            pltpu.VMEM((JP, HD), F32),
            pltpu.VMEM((KVH - 1, 2, VT16, HD), BF16),
            pltpu.VMEM((KVH - 1, 2, VT16, HD), BF16),
            pltpu.VMEM((2, VT16, HD), BF16),
            pltpu.VMEM((2, VT16, HD), BF16),
        ]
        + [
            pltpu.SemaphoreType.DMA((4,)),
            pltpu.SemaphoreType.DMA((2, STEPS)),
            pltpu.SemaphoreType.DMA((4,)),
            pltpu.SemaphoreType.DMA((2, STEPS)),
        ]
        + [pltpu.SemaphoreType.DMA((KVH - 1,))] * 2
        + [pltpu.SemaphoreType.DMA] * 2
        + [
            pltpu.SemaphoreType.DMA((2,)),
            pltpu.SemaphoreType.DMA((2,)),
            pltpu.SemaphoreType.DMA((2,)),
            pltpu.SemaphoreType.DMA((2,)),
            pltpu.SemaphoreType.DMA((4,)),
            pltpu.SemaphoreType.DMA,
        ],
        compiler_params=pltpu.CompilerParams(
            collective_id=0, has_side_effects=True, vmem_limit_bytes=62 * 1024 * 1024
        ),
    )(reads.T, q, g, keys, values, keys, values)
    attended, grad_queries, grad_keys, grad_values = pl.pallas_call(
        copy_out,
        out_shape=tuple(jax.ShapeDtypeStruct(r.shape, r.dtype) for r in results[:4]),
        in_specs=[hbm] * 7,
        out_specs=(hbm,) * 4,
        scratch_shapes=[pltpu.SMEM((8, 128), jnp.int32)]
        + [pltpu.VMEM(r.shape, r.dtype) for r in results]
        + [pltpu.SemaphoreType.DMA((9,)), pltpu.SemaphoreType.DMA((6,))],
    )(reads.T, *results)
    return (
        attended.reshape(queries.shape),
        grad_queries.reshape(queries.shape),
        jnp.swapaxes(grad_keys, 1, 2),
        jnp.swapaxes(grad_values, 1, 2),
    )


def solution(mesh):
    placed = (
        P(("seq", "enc"), None),
        P("enc", None, None),
        P("enc", None, None),
        P(),
        P(("seq", "enc"), None),
    )
    return jax.shard_map(
        per_device,
        mesh=mesh,
        in_specs=placed,
        out_specs=(
            P(("seq", "enc"), None),
            P(("seq", "enc"), None),
            P("enc", None, "seq"),
            P("enc", None, "seq"),
        ),
        check_vma=False,
    )
```
